256 devices in a mesh: expert: 32 (over z, x), dp: 8 (over y, core).
Axes of the slice: x: 4, y: 4, z: 8, core: 2. Of those that a mesh axis runs over, the one named last changes fastest.
Arguments:
- upper_out: float32 [32768, 2048], P(('expert', 'dp')), may hold values from -3 to 3
- lower_out: bfloat16 [32768, 2048], P(('expert', 'dp')), may hold values from -6 to 6
- upper_cot: bfloat16 [32768, 2048], P(('expert', 'dp')), may hold values from -6 to 6
- lower_cot: bfloat16 [32768, 2048], P(('expert', 'dp')), may hold values from -3 to 3
- gate_up_weight: bfloat16 [32, 2048, 1408], P('expert', 'dp'), may hold values from -0.125 to 0.125
- down_weight: bfloat16 [32, 2048, 704], P('expert', 'dp'), may hold values from -0.21875 to 0.21875
- router_weight: float32 [2048, 32], replicated, may hold values from -0.125 to 0.125
- expert_ids: int32 [32768, 2], P(('expert', 'dp')), may hold values from 0 to 31, all different within a row; in each aligned block of 128 rows (0 to 127, 128 to 255, ...) at most 9 rows name the same one
- keep_mask: int32 [32768, 2], P(('expert', 'dp')), may hold values 0 or 1
Outputs:
- upper_input: float32 [32768, 2048], P(('expert', 'dp'))
- lower_grad: float32 [32768, 2048], P(('expert', 'dp'))
- gate_up_grad: bfloat16 [32, 2048, 1408], P('expert', 'dp')
- down_grad: bfloat16 [32, 2048, 704], P('expert', 'dp')
- router_grad: float32 [2048, 32], replicated
The draws below stay inside these ranges and needn't reach their ends.
Inputs may be any that keep to these rules, and one draw needn't show every extreme that they name: `expert_ids`: each row names 2 different experts. Within the rows of one device (aligned blocks of 128 rows) no expert is named by more than 9 rows, a bound that some block reaches.
All inputs are finite; a program needn't handle non-finite values. No bound on the sum of `keep_mask` on one device may be relied on, other than what follows from the above.
Results may differ from the reference program's by a relative error of at most 0.017.
Values may be sent and summed in bfloat16 or wider, within the bound.
No kernel may reach another device: no remote copies, remote signals or barrier semaphores. Data moves between devices by JAX's collectives and lax.ppermute only.
A program may use at most 128 MiB of HBM per device.

```python
import math
import jax
import jax.numpy as jnp
import numpy as np
from jax import lax

HALF = 2048
FF = 704
TOP = 2
TOK_DEV = 128
EXPERTS = 32
CAP = 9
TOKENS = 32768
N_EXPERT = 32
N_DP = 8


def place_ends(drawn, stream_key, low, high):
    shape = drawn.shape
    place = [jax.random.randint(jax.random.fold_in(stream_key, axis), (), 0, shape[axis]) for axis in range(len(shape))]
    drawn = drawn.at[tuple(place)].set(low)
    longest = shape.index(max(shape))
    place[longest] = (place[longest] + 1) % shape[longest]
    return drawn.at[tuple(place)].set(high)


def levels(stream_key, extent, shards, low, largest):
    gain, own = 1.0, jax.random.fold_in(stream_key, 6)
    for dim, parts in shards:
        draws = jnp.exp(jax.random.uniform(jax.random.fold_in(own, dim), (parts,), jnp.float32, low / len(shards), largest / len(shards)))
        gain = gain * jnp.repeat(draws, extent[dim] // parts).reshape([-1 if axis == dim else 1 for axis in range(len(extent))])
    return gain


def assign_block(own_key, own, number, rows, amount, top, bound, lean):
    ranking = jax.random.permutation(own_key, amount)
    packed, common = shares(amount, rows * top, bound, lean, True), shares(amount, rows * top, bound, lean, False)
    places = jnp.arange(amount)

    def named(sizes, rotation):
        used = int((sizes > 0).sum())
        fixed = max(1, used // 4)
        moved = fixed + (places - fixed + rotation * (used - fixed)) % max(1, amount - fixed)
        return jnp.zeros((amount,), jnp.int32).at[ranking[jnp.where(places < fixed, places, moved)]].set(jnp.asarray(sizes, jnp.int32))

    sizes = jnp.where(number % 4 == 0, named(packed, number // 4), named(common, number - number // 4 - 1))
    mixed = jax.random.permutation(jax.random.fold_in(own, 3), amount)
    source_of, receiver = mixed[0:amount // 2 * 2:2], mixed[1:amount // 2 * 2:2]
    room = jnp.minimum(sizes[source_of] - 1, bound - sizes[receiver]) // 2
    room = jnp.where((source_of == ranking[0]) | (receiver == ranking[0]) | (sizes[receiver] == 0), 0, jnp.maximum(room, 0))
    moved = jax.random.randint(jax.random.fold_in(own, 4), (amount // 2,), 0, 1 << 20) % (room + 1)
    sizes = sizes.at[source_of].add(-moved).at[receiver].add(moved)
    members = jnp.searchsorted(jnp.cumsum(sizes), jnp.arange(rows * top), side="right").astype(jnp.int32)
    grid = members.reshape(top, rows).T
    grid = grid[jax.random.permutation(jax.random.fold_in(own, 1), rows)]
    rotation = jax.random.randint(jax.random.fold_in(own, 2), (rows, 1), 0, top)
    return jnp.take_along_axis(grid, (jnp.arange(top)[None, :] + rotation) % top, axis=1)


def shares(count, total, most, lean, full):
    weights = [(1 << 20) // math.isqrt(standing ** lean) + 1 for standing in range(1, count + 1)]
    largest = most if full else min(most, max(-(-total // count), total * weights[0] // sum(weights)))
    least = 1 if total - largest >= count - 1 else 0
    holding, surplus = [largest] + [least] * (count - 1), total - largest - least * (count - 1)
    while surplus > 0:
        candidates = [i for i in range(1, count) if holding[i] < largest] or [i for i in range(1, count) if holding[i] < most]
        pool, budget = sum([weights[i] for i in candidates]), surplus
        for i in candidates:
            extra = min(most - holding[i], max(1, budget * weights[i] // pool), surplus)
            holding[i] = holding[i] + extra
            surplus = surplus - extra
    return np.array(holding)


def gaussian(key, extent, width, most, pieces=(), kind=jnp.bfloat16):
    loudness = levels(key, extent, pieces, -0.22, 0.18) if pieces else 1.0
    result = jax.random.normal(key, extent, jnp.float32) * width * loudness
    return jnp.minimum(jnp.maximum(result, -most), most).astype(kind)


def setup_inputs(seed: int = 0) -> dict:
    key_list = jax.random.split(jax.random.key(seed), 10)
    upper_out = gaussian(key_list[0], (TOKENS, HALF), 0.5, 3.0, ((0, 256),), jnp.float32)
    lower_out = gaussian(key_list[1], (TOKENS, HALF), 1.0, 6.0, ((0, 256),))
    upper_cot = gaussian(key_list[2], (TOKENS, HALF), 1.0, 6.0, ((0, 256),))
    lower_cot = gaussian(key_list[3], (TOKENS, HALF), 0.5, 3.0, ((0, 256),))
    gate_up_weight = gaussian(key_list[4], (EXPERTS, HALF, 2 * FF), HALF ** -0.5, 0.125, ((0, 32), (1, 8)))
    down_weight = gaussian(key_list[5], (EXPERTS, HALF, FF), FF ** -0.5, 0.21875, ((0, 32), (1, 8)))
    router_weight = gaussian(key_list[6], (HALF, EXPERTS), HALF ** -0.5, 0.125, (), jnp.float32)
    expert_ids_keys = jax.random.split(jax.random.fold_in(key_list[7], 1), TOKENS // TOK_DEV)
    expert_ids_turns = jax.random.permutation(jax.random.fold_in(key_list[7], 3), TOKENS // TOK_DEV)
    expert_ids = jax.vmap(lambda own, number: assign_block(jax.random.fold_in(key_list[7], 2), own, number, TOK_DEV, EXPERTS, TOP, CAP, 2))(expert_ids_keys, expert_ids_turns).reshape((TOKENS, TOP))
    keep_mask = place_ends((jax.random.randint(key_list[8], (TOKENS, TOP), 0, 8) < 7).astype(jnp.int32), jax.random.fold_in(key_list[8], 1), 0, 1)
    return {"upper_out": upper_out, "lower_out": lower_out, "upper_cot": upper_cot, "lower_cot": lower_cot, "gate_up_weight": gate_up_weight, "down_weight": down_weight, "router_weight": router_weight, "expert_ids": expert_ids, "keep_mask": keep_mask}


residual_scale = 128.0 ** -0.5
highest = lax.Precision.HIGHEST


def expert_pass(row_block, grads, gate_up, down):
    hidden_units = down.shape[1]
    projected = jnp.dot(row_block, gate_up, preferred_element_type=jnp.float32)
    gate_part = projected[:, :hidden_units]
    up_part = projected[:, hidden_units:]
    gate_sig = jax.nn.sigmoid(gate_part)
    activated = gate_part * gate_sig
    hidden = (activated * up_part).astype(jnp.bfloat16)
    outputs = lax.dot_general(hidden, down, (((1,), (1,)), ((), ())), preferred_element_type=jnp.float32).astype(jnp.bfloat16)
    down_part = lax.dot_general(grads, hidden, (((0,), (0,)), ((), ())), preferred_element_type=jnp.float32)
    hidden_grad = jnp.dot(grads, down, preferred_element_type=jnp.float32)
    gate_grad = hidden_grad * up_part * (gate_sig * (1.0 + gate_part * (1.0 - gate_sig)))
    up_grad = hidden_grad * activated
    joined = jnp.concatenate([gate_grad, up_grad], axis=1).astype(jnp.bfloat16)
    gate_up_part = lax.dot_general(row_block, joined, (((0,), (0,)), ((), ())), preferred_element_type=jnp.float32)
    rows_grad = lax.dot_general(joined, gate_up, (((1,), (1,)), ((), ())), preferred_element_type=jnp.float32).astype(jnp.bfloat16)
    return outputs, rows_grad, gate_up_part, down_part


def pick_rows(table, index):
    return table[index]


def reference(upper_out, lower_out, upper_cot, lower_cot, gate_up_weight, down_weight, router_weight, expert_ids, keep_mask):
    blocks = N_EXPERT * N_DP
    assign = TOK_DEV * TOP
    slots = EXPERTS * CAP
    expert_range = jnp.arange(EXPERTS, dtype=jnp.int32)
    block_ids = expert_ids.reshape(blocks, assign)
    block_kept = keep_mask.reshape(blocks, assign)
    onehot = (block_ids[:, :, None] == expert_range).astype(jnp.int32)
    slot_rank = jnp.sum(onehot * (jnp.cumsum(onehot, axis=1) - 1), axis=2)
    slot_pos = (block_ids * CAP + slot_rank).astype(jnp.int32)

    def invert(positions):
        return jnp.full((slots,), assign, jnp.int32).at[positions].set(jnp.arange(assign, dtype=jnp.int32))

    slot_src = jax.vmap(invert)(slot_pos)
    kept_ext = jnp.concatenate([block_kept, jnp.zeros((blocks, 1), jnp.int32)], axis=1)
    slot_kept = jnp.take_along_axis(kept_ext, slot_src, axis=1)
    slot_tok = jnp.where(slot_kept > 0, slot_src // TOP, TOK_DEV).astype(jnp.int32)

    logits = jnp.dot(lower_out.astype(jnp.float32), router_weight, precision=highest)
    pair_hot = (expert_ids[:, :, None] == expert_range).astype(jnp.float32)
    chosen = jnp.sum(pair_hot * logits[:, None, :], axis=2)
    first_share = jax.nn.sigmoid(chosen[:, 0] - chosen[:, 1])
    weight = jnp.stack([first_share, 1.0 - first_share], axis=1) * keep_mask.astype(jnp.float32)
    weight_ext = jnp.concatenate([weight.reshape(blocks, assign), jnp.zeros((blocks, 1), jnp.float32)], axis=1)
    slot_weight = jnp.take_along_axis(weight_ext, slot_src, axis=1)

    lower_ext = jnp.concatenate([lower_out.reshape(blocks, TOK_DEV, HALF), jnp.zeros((blocks, 1, HALF), jnp.bfloat16)], axis=1)
    send_rows = jax.vmap(pick_rows)(lower_ext, slot_tok)
    cot_ext = jnp.concatenate([upper_cot.reshape(blocks, TOK_DEV, HALF), jnp.zeros((blocks, 1, HALF), jnp.bfloat16)], axis=1)
    send_cot = (jax.vmap(pick_rows)(cot_ext, slot_tok).astype(jnp.float32) * (residual_scale * slot_weight)[:, :, None]).astype(jnp.bfloat16)

    def regroup(array):
        return jnp.transpose(array.reshape(N_EXPERT, N_DP, EXPERTS, CAP, HALF), (2, 1, 0, 3, 4)).reshape(EXPERTS, N_DP, N_EXPERT * CAP, HALF)

    def ungroup(array):
        return jnp.transpose(array.reshape(EXPERTS, N_DP, N_EXPERT, CAP, HALF), (2, 1, 0, 3, 4)).reshape(blocks, slots, HALF)

    def per_expert(inputs):
        rows_all, grads_all, gate_up, down = inputs

        def step(totals, pair_in):
            outputs, rows_grad, gate_up_part, down_part = expert_pass(pair_in[0], pair_in[1], gate_up, down)
            first = totals[0] + lax.optimization_barrier(gate_up_part.astype(jnp.bfloat16)).astype(jnp.float32)
            second = totals[1] + lax.optimization_barrier(down_part.astype(jnp.bfloat16)).astype(jnp.float32)
            return (first, second), (outputs, rows_grad)

        init = (jnp.zeros((HALF, 2 * FF), jnp.float32), jnp.zeros((HALF, FF), jnp.float32))
        totals, stacked = lax.scan(step, init, (rows_all, grads_all))
        return totals[0].astype(jnp.bfloat16), totals[1].astype(jnp.bfloat16), stacked[0], stacked[1]

    gate_up_grad, down_grad, expert_out, rows_back = lax.map(per_expert, (regroup(send_rows), regroup(send_cot), gate_up_weight, down_weight))
    out_assign = jax.vmap(pick_rows)(ungroup(expert_out), slot_pos).astype(jnp.float32).reshape(TOKENS, TOP, HALF)
    back_assign = jax.vmap(pick_rows)(ungroup(rows_back), slot_pos).astype(jnp.float32).reshape(TOKENS, TOP, HALF)

    mixed = jnp.sum(weight[:, :, None] * out_assign, axis=1)
    upper_input = upper_out - residual_scale * mixed
    share_grad = residual_scale * keep_mask.astype(jnp.float32) * jnp.sum(upper_cot.astype(jnp.float32)[:, None, :] * out_assign, axis=2)
    diff_grad = (share_grad[:, 0] - share_grad[:, 1]) * first_share * (1.0 - first_share)
    logit_grad = diff_grad[:, None] * (pair_hot[:, 0] - pair_hot[:, 1])
    lower_grad = lower_cot.astype(jnp.float32) + jnp.sum(back_assign, axis=1) + jnp.dot(logit_grad, router_weight.T, precision=highest)
    router_grad = jnp.dot(lower_out.astype(jnp.float32).T, logit_grad, precision=highest)
    return upper_input, lower_grad, gate_up_grad, down_grad, router_grad
```

```python
import jax
import jax.numpy as jnp
from jax import lax
from jax.sharding import PartitionSpec as P

residual_scale = 128.0 ** (-0.5)
highest = lax.Precision.HIGHEST
contract_last = (((1,), (1,)), ((), ()))
contract_first = (((0,), (0,)), ((), ()))
f32, bf16 = jnp.float32, jnp.bfloat16
fold = 8


def exchange(array):
    return lax.all_to_all(array, "expert", split_axis=0, concat_axis=0, tiled=True)


def pack(rows, experts, extra=()):
    features = rows.shape[1]
    main = experts * fold
    parts = [rows[:main].reshape(experts, fold, features)]
    for start in range(main, rows.shape[0], experts):
        parts.append(rows[start : start + experts].reshape(experts, fold, features // fold))
    return jnp.concatenate([*parts, *extra], axis=2)


def unpack(block, features):
    experts, _, width = block.shape
    rows = [block[:, :, :features].reshape(experts * fold, features)]
    for start in range(features, width - features // fold + 1, features // fold):
        rows.append(block[:, :, start : start + features // fold].reshape(experts, features))
    return jnp.concatenate(rows, axis=0)


def body(
    upper_out,
    lower_out,
    upper_cot,
    lower_cot,
    gate_up_weight,
    down_weight,
    router_weight,
    expert_ids,
    keep_mask,
):
    tokens, features = lower_out.shape
    experts = router_weight.shape[1]
    hidden_units = down_weight.shape[2]
    main = experts * fold
    slots = main + experts
    gate_up = lax.all_gather(gate_up_weight[0], "dp", axis=0, tiled=True)
    down = lax.all_gather(down_weight[0], "dp", axis=0, tiled=True)

    expert_range = jnp.arange(experts, dtype=jnp.int32)
    hot = [(expert_ids[:, k, None] == expert_range).astype(f32) for k in range(2)]
    earlier = (
        jnp.arange(tokens, dtype=jnp.int32)[:, None] > jnp.arange(tokens, dtype=jnp.int32)
    ).astype(bf16)
    counts = jnp.dot(earlier, (hot[0] + hot[1]).astype(bf16), preferred_element_type=f32)
    place = []
    for k in range(2):
        rank = jnp.sum(hot[k] * counts, axis=1).astype(jnp.int32)
        slot = jnp.where(rank < fold, expert_ids[:, k] * fold + rank, main + expert_ids[:, k])
        place.append(slot[:, None] == jnp.arange(slots, dtype=jnp.int32))
    kept = keep_mask.astype(f32)
    used = jnp.where(place[0], kept[:, :1], 0.0) + jnp.where(place[1], kept[:, 1:], 0.0)
    used = used.astype(bf16)
    rows = lax.dot_general(used, lower_out, contract_first, preferred_element_type=f32)
    arrived = exchange(pack(rows.astype(bf16), experts))

    logits = jnp.dot(lower_out.astype(f32), router_weight, precision=highest)
    gap = jnp.sum((hot[0] - hot[1]) * logits, axis=1)
    share = jax.nn.sigmoid(gap)
    rest = 1.0 - share
    weights = (share * kept[:, 0], rest * kept[:, 1])
    mix = jnp.where(place[0], weights[0][:, None], 0.0) + jnp.where(
        place[1], weights[1][:, None], 0.0
    )
    slot_weight = jnp.sum(mix, axis=0)
    cot_rows = lax.dot_general(used, upper_cot, contract_first, preferred_element_type=f32)
    cot_rows = (cot_rows * (residual_scale * slot_weight)[:, None]).astype(bf16)
    partner = jnp.sum(
        jnp.where(place[0], expert_ids[:, 1:].astype(f32), 0.0)
        + jnp.where(place[1], expert_ids[:, :1].astype(f32), 0.0),
        axis=0,
    )
    other = jnp.sum(
        jnp.where(place[0], rest[:, None], 0.0) + jnp.where(place[1], share[:, None], 0.0), axis=0
    )
    other_high = lax.reduce_precision(other, 8, 7)
    facts = jnp.stack([partner, other_high, other - other_high], axis=1).astype(bf16)
    facts = jnp.concatenate(
        [
            facts[:main].reshape(experts, fold, 3),
            jnp.broadcast_to(facts[main:, None, :], (experts, fold, 3)),
        ],
        axis=2,
    )
    facts = jnp.pad(facts, ((0, 0), (0, 0), (0, 122)))
    cot_arrived = exchange(pack(cot_rows, experts, (facts,)))

    row_block = unpack(arrived, features)
    projected = jnp.dot(row_block, gate_up, preferred_element_type=f32)
    gate_part = projected[:, :hidden_units]
    up_part = projected[:, hidden_units:]
    gate_sig = jax.nn.sigmoid(gate_part)
    activated = gate_part * gate_sig
    hidden = (activated * up_part).astype(bf16)
    outputs = lax.dot_general(hidden, down, contract_last, preferred_element_type=f32).astype(bf16)

    grads = unpack(cot_arrived[:, :, : features + features // fold], features)
    facts = cot_arrived[:, :, features + features // fold :]
    facts = jnp.concatenate([facts[:, :, :3].reshape(main, 3), facts[:, 0, 3:6]], axis=0)
    facts = facts.astype(f32)
    inner = jnp.sum(grads.astype(f32) * outputs.astype(f32), axis=1)
    change = inner * (facts[:, 1] + facts[:, 2])
    own = lax.axis_index("expert")
    sign = (expert_range == own).astype(f32) - (
        facts[:, 0].astype(jnp.int32)[:, None] == expert_range
    ).astype(f32)
    logit_grad = change[:, None] * sign
    router_part = lax.dot_general(
        logit_grad, row_block.astype(f32), contract_first, precision=highest
    )
    out_back = exchange(
        pack(jnp.concatenate([outputs, router_part.astype(bf16)], axis=0), experts)
    )

    hidden_grad = jnp.dot(grads, down, preferred_element_type=f32)
    gate_grad = hidden_grad * up_part * (gate_sig * (1.0 + gate_part * (1.0 - gate_sig)))
    up_grad = hidden_grad * activated
    joined = jnp.concatenate([gate_grad, up_grad], axis=1).astype(bf16)
    down_part = lax.dot_general(grads, hidden, contract_first, preferred_element_type=f32)
    gate_up_part = lax.dot_general(row_block, joined, contract_first, preferred_element_type=f32)
    both = jnp.concatenate([gate_up_part.astype(bf16), down_part.astype(bf16)], axis=1)
    both = lax.psum_scatter(both, "dp", scatter_dimension=0, tiled=True)
    rows_grad = lax.dot_general(joined, gate_up, contract_last, preferred_element_type=f32)
    rows_grad = rows_grad + jnp.dot(logit_grad, router_weight.T, precision=highest)
    rows_back = exchange(pack(rows_grad.astype(bf16), experts))

    out_rows = unpack(out_back, features)
    router_row = jnp.sum(out_rows[slots:].astype(f32), axis=0)
    router_row = jnp.sum(lax.all_gather(router_row.reshape(fold, -1), "dp"), axis=0)
    router_all = exchange(jnp.broadcast_to(router_row, (experts, *router_row.shape)))
    router_grad = router_all.reshape(experts, features).T
    mixed = jnp.dot(mix, out_rows[:slots].astype(f32), precision=highest)
    upper_input = upper_out - residual_scale * mixed
    back = jnp.dot(
        (place[0] | place[1]).astype(bf16), unpack(rows_back, features), preferred_element_type=f32
    )
    lower_grad = lower_cot.astype(f32) + back
    return (
        upper_input,
        lower_grad,
        both[None, :, : 2 * hidden_units],
        both[None, :, 2 * hidden_units :],
        router_grad,
    )


def solution(mesh):
    blocks = P(("expert", "dp"), None)
    split = P("expert", "dp", None)
    return jax.shard_map(
        body,
        mesh=mesh,
        in_specs=(blocks, blocks, blocks, blocks, split, split, P(), blocks, blocks),
        out_specs=(blocks, blocks, split, split, P()),
        check_vma=False,
    )
```

```python
import jax
import jax.numpy as jnp
from jax import lax
from jax.experimental import pallas as pl
from jax.experimental.pallas import tpu as pltpu
from jax.sharding import PartitionSpec as P

residual_scale = 128.0 ** (-0.5)
highest = lax.Precision.HIGHEST
contract_last = (((1,), (1,)), ((), ()))
contract_first = (((0,), (0,)), ((), ()))
f32, bf16, i32 = jnp.float32, jnp.bfloat16, jnp.int32
fold = 8
facts_width = 128


def dot(left, right, dims=(((1,), (0,)), ((), ()))):
    return lax.dot_general(left, right, dims, preferred_element_type=f32)


def call(kernel, shapes, cost, aliases=None, **specs):
    return pl.pallas_call(
        kernel,
        out_shape=shapes,
        input_output_aliases=aliases or {},
        cost_estimate=pl.CostEstimate(flops=cost, bytes_accessed=0, transcendentals=0),
        compiler_params=pltpu.CompilerParams(vmem_limit_bytes=48 * 2**20),
        **specs,
    )


def places(ids, experts):
    tokens = ids.shape[1]
    rows = lax.broadcasted_iota(i32, (experts, tokens), 0)
    hot = [(rows == ids[k : k + 1, :]).astype(f32) for k in range(2)]
    earlier = lax.broadcasted_iota(i32, (tokens, tokens), 0) < lax.broadcasted_iota(
        i32, (tokens, tokens), 1
    )
    counts = dot((hot[0] + hot[1]).astype(bf16), earlier.astype(f32).astype(bf16))
    slots = []
    for k in range(2):
        rank = jnp.sum(hot[k] * counts, axis=0, keepdims=True).astype(i32)
        slots.append(
            jnp.where(rank < fold, ids[k : k + 1, :] * fold + rank, -1 - ids[k : k + 1, :])
        )
    return hot, slots


def spread(slots, values, experts):
    tokens = slots[0].shape[1]
    rows = lax.broadcasted_iota(i32, (experts * fold, tokens), 0)
    ninth = -1 - rows // fold
    zero = jnp.zeros((), f32)
    main = sum(jnp.where(rows == slots[k], values[k], zero) for k in range(2))
    extra = sum(jnp.where(ninth == slots[k], values[k], zero) for k in range(2))
    return main, extra


def gather_rows(main, extra, table, scale_main, scale_extra, out):
    count, features = main.shape[0], table.shape[1]
    part = features // fold
    own = lax.broadcasted_iota(i32, extra.shape, 0) % fold
    main = main.astype(bf16)
    total = jnp.zeros((count, part), f32)
    for c in range(fold):
        piece = table[:, c * part : (c + 1) * part]
        rows = dot(main, piece)
        if scale_main is not None:
            rows = rows * scale_main
        out[:, c * part : (c + 1) * part] = rows.astype(bf16)
        total += dot(jnp.where(own == c, extra, 0.0).astype(bf16), piece)
    if scale_extra is not None:
        total = total * scale_extra
    out[:, features : features + part] = total.astype(bf16)


def send_rows_kernel(experts, ids, keep, table, out):
    _, slots = places(ids[...], experts)
    kept = keep[...].astype(f32)
    main, extra = spread(slots, (kept[:1], kept[1:]), experts)
    gather_rows(main, extra, table, None, None, out)


def send_cot_kernel(experts, ids, keep, lower, cot, router, out, mix, used):
    ids_now = ids[...]
    features = lower.shape[1]
    part = features // fold
    hot, slots = places(ids_now, experts)
    kept = keep[...].astype(f32)
    logits = lax.dot_general(
        router[...],
        lower[...].astype(f32),
        contract_last,
        precision=highest,
        preferred_element_type=f32,
    )
    gap = jnp.sum((hot[0] - hot[1]) * logits, axis=0, keepdims=True)
    share = jax.nn.sigmoid(gap)
    rest = 1.0 - share
    used_main, used_extra = spread(slots, (kept[:1], kept[1:]), experts)
    mix_main, mix_extra = spread(slots, (share * kept[:1], rest * kept[1:]), experts)
    weight_main = jnp.sum(mix_main, axis=1, keepdims=True) * residual_scale
    weight_extra = jnp.sum(mix_extra, axis=1, keepdims=True) * residual_scale
    gather_rows(used_main, used_extra, cot, weight_main, weight_extra, out)
    partner = spread(slots, (ids_now[1:].astype(f32), ids_now[:1].astype(f32)), experts)
    other = spread(slots, (rest, share), experts)
    lane = lax.broadcasted_iota(i32, (experts * fold, facts_width), 1)
    facts = jnp.zeros((experts * fold, facts_width), f32)
    for k in range(2):
        number = jnp.sum(partner[k], axis=1, keepdims=True)
        factor = jnp.sum(other[k], axis=1, keepdims=True)
        high = factor.astype(bf16).astype(f32)
        for place, value in enumerate((number, high, factor - high)):
            facts = jnp.where(lane == 3 * k + place, value, facts)
    out[:, features + part :] = facts.astype(bf16)
    width = experts * fold
    for k, value in enumerate((mix_main, mix_extra)):
        value = value.T
        high = value.astype(bf16)
        mix[:, 2 * k * width : (2 * k + 1) * width] = high
        mix[:, (2 * k + 1) * width : (2 * k + 2) * width] = (value - high.astype(f32)).astype(bf16)
    for k, value in enumerate((used_main, used_extra)):
        used[:, k * width : (k + 1) * width] = value.T.astype(bf16)


def signs(facts, change, own, column, experts):
    count = change.shape[0]
    col = lax.broadcasted_iota(i32, (count, experts * fold), 1) // fold
    partner = facts[:, column : column + 1].astype(i32)
    return jnp.where(col == own, change, 0.0) - jnp.where(col == partner, change, 0.0)


def router_kernel(experts, own, cot, rows, sent, out, grad):
    count = cot.shape[0]
    features = (rows.shape[1] * fold) // (fold + 1)
    part = features // fold
    total = jnp.zeros((count, 128), f32)
    for start in range(0, features, 128):
        total += cot[:, start : start + 128].astype(f32) * sent[:, start : start + 128].astype(f32)
    extra = jnp.zeros((count, 128), f32)
    for start in range(features, features + part, 128):
        extra += cot[:, start : start + 128].astype(f32) * sent[:, start : start + 128].astype(f32)
    extra = extra.reshape(experts, fold, 128)
    extra = jnp.broadcast_to(jnp.sum(extra, axis=1, keepdims=True), extra.shape)
    facts = cot[:, features + part :].astype(f32)
    changes = []
    for k, value in enumerate((total, extra.reshape(count, 128))):
        inner = jnp.sum(value, axis=1, keepdims=True)
        change = inner * (facts[:, 3 * k + 1 : 3 * k + 2] + facts[:, 3 * k + 2 : 3 * k + 3])
        changes.append(signs(facts, change, own[0], 3 * k, experts))
    row = lax.broadcasted_iota(i32, (count, count), 0) % fold
    lane = lax.broadcasted_iota(i32, (count, count), 1) % fold
    result = jnp.zeros((count, part), f32)
    for c in range(fold):
        left = jnp.where(lane == c, changes[0], 0.0).astype(bf16)
        result += dot(left, rows[:, c * part : (c + 1) * part], contract_first)
        left = jnp.where((lane == c) & (row == c), changes[1], 0.0).astype(bf16)
        result += dot(left, rows[:, features : features + part], contract_first)
    out[...] = result.astype(bf16)
    pick = lax.broadcasted_iota(i32, (count, 128), 0) == fold * lax.broadcasted_iota(
        i32, (count, 128), 1
    )
    pick = pick.astype(f32).astype(bf16)
    for k in range(2):
        high = changes[k].astype(bf16)
        low = (changes[k] - high.astype(f32)).astype(bf16)
        grad[k] = dot(high, pick) + dot(low, pick)


def upper_kernel(upper, back, mix, out):
    features = upper.shape[1]
    part = features // fold
    width = mix.shape[1] // 4
    lane = lax.broadcasted_iota(i32, (mix.shape[0], width), 1) % fold
    main_high, main_low = mix[:, :width], mix[:, width : 2 * width]
    extra_high = mix[:, 2 * width : 3 * width].astype(f32)
    extra_low = mix[:, 3 * width :].astype(f32)
    folded = back[:, features : features + part]
    for c in range(fold):
        piece = back[:, c * part : (c + 1) * part]
        mixed = dot(main_high, piece) + dot(main_low, piece)
        mixed += dot(jnp.where(lane == c, extra_high, 0.0).astype(bf16), folded)
        mixed += dot(jnp.where(lane == c, extra_low, 0.0).astype(bf16), folded)
        out[:, c * part : (c + 1) * part] = (
            upper[:, c * part : (c + 1) * part] - residual_scale * mixed
        )


def lower_kernel(lower_cot, back, used, out):
    features = lower_cot.shape[1]
    part = features // fold
    width = used.shape[1] // 2
    lane = lax.broadcasted_iota(i32, (used.shape[0], width), 1) % fold
    main, extra = used[:, :width], used[:, width:].astype(f32)
    folded = back[:, features : features + part]
    for c in range(fold):
        rows = dot(main, back[:, c * part : (c + 1) * part])
        rows += dot(jnp.where(lane == c, extra, 0.0).astype(bf16), folded)
        out[:, c * part : (c + 1) * part] = (
            lower_cot[:, c * part : (c + 1) * part].astype(f32) + rows
        )


def hidden_kernel(experts, cot, projected, down, joined, rows):
    features = down.shape[1]
    part = features // fold
    main = experts * fold
    units = down.shape[0]
    order = lax.broadcasted_iota(i32, (main, main), 1)
    place = lax.broadcasted_iota(i32, (main, main), 0)
    order = order == (place % experts) * fold + place // experts
    extra = dot(order.astype(f32).astype(bf16), cot[:, features : features + part]).astype(bf16)
    rows[:main, :] = cot[:, :features]
    for c in range(fold):
        rows[main:, c * part : (c + 1) * part] = extra[c * experts : (c + 1) * experts]
    back = dot(rows[...], down[...], contract_last)
    gate, up = projected[:, :units], projected[:, units:]
    gate_sig = jax.nn.sigmoid(gate)
    activated = gate * gate_sig
    joined[:, :units] = (back * up * (gate_sig * (1.0 + gate * (1.0 - gate_sig)))).astype(bf16)
    joined[:, units:] = (back * activated).astype(bf16)


def outputs_kernel(experts, hidden, down, out, total):
    step = pl.program_id(0)
    main = experts * fold

    @pl.when(step == 0)
    def _():
        total[...] = jnp.zeros_like(total)

    @pl.when(step < fold)
    def _():
        result = dot(hidden[...], down[...])
        out[...] = result[:main].astype(bf16)
        total[...] += unfolded(result[main:].astype(bf16), step, experts)

    @pl.when(step == fold)
    def _():
        out[...] = total[...].astype(bf16)

    @pl.when(step > fold)
    def _():
        out[...] = jnp.zeros_like(out)


def unfolded(extra, step, experts):
    row = lax.broadcasted_iota(i32, (experts * fold, experts), 0)
    lane = lax.broadcasted_iota(i32, (experts * fold, experts), 1)
    return dot((row == lane * fold + step).astype(f32).astype(bf16), extra)


def rows_kernel(experts, joined, gate_up, grad, router, out, total):
    step = pl.program_id(0)
    main = experts * fold

    @pl.when(step == 0)
    def _():
        total[...] = jnp.zeros_like(total)

    @pl.when(step < fold)
    def _():
        result = dot(joined[...], gate_up[...], contract_last)
        change = lax.dot_general(
            grad[...].reshape(2 * main, grad.shape[2])[:, :experts],
            router[...],
            (((1,), (0,)), ((), ())),
            precision=highest,
            preferred_element_type=f32,
        )
        out[...] = (result[:main] + change[:main]).astype(bf16)
        own = lax.broadcasted_iota(i32, (main, out.shape[1]), 0) % fold == step
        extra = result[main:]
        high = extra.astype(bf16)
        low = (extra - high.astype(f32)).astype(bf16)
        total[...] += (
            unfolded(high, step, experts)
            + unfolded(low, step, experts)
            + jnp.where(own, change[main:], 0.0)
        )

    @pl.when(step == fold)
    def _():
        out[...] = total[...].astype(bf16)


def reduce_kernel(back, out):
    folded = back[...].astype(f32).reshape(back.shape[0] // fold, *out.shape)
    out[...] = jnp.sum(folded, axis=0)


def grads_kernel(rows, joined, cot, hidden, out):
    wide = joined.shape[1]
    out[:, :wide] = dot(rows[...], joined[...], contract_first).astype(bf16)
    out[:, wide:] = dot(cot[...], hidden[...], contract_first).astype(bf16)


def exchange(array, experts):
    width = array.shape[1]
    moved = lax.all_to_all(
        array.reshape(experts, fold, width), "expert", split_axis=0, concat_axis=0, tiled=True
    )
    return moved.reshape(experts * fold, width)


def unpack(block, features, experts):
    part = features // fold
    extra = block[:, features : features + part].reshape(experts, features)
    return jnp.concatenate([block[:, :features], extra], axis=0)


def body(
    upper_out,
    lower_out,
    upper_cot,
    lower_cot,
    gate_up_weight,
    down_weight,
    router_weight,
    expert_ids,
    keep_mask,
):
    tokens, features = lower_out.shape
    experts = router_weight.shape[1]
    hidden_units = down_weight.shape[2]
    main = experts * fold
    part = features // fold
    ids, keep, router = expert_ids.T, keep_mask.T, router_weight.T
    gate_up = lax.all_gather(gate_up_weight[0], "dp", axis=0, tiled=True)
    down = lax.all_gather(down_weight[0].T, "dp", axis=1, tiled=True)
    whole = pl.BlockSpec(memory_space=pltpu.VMEM)
    scalar = pl.BlockSpec(memory_space=pltpu.SMEM)

    def shape(*dims, kind=bf16):
        return jax.ShapeDtypeStruct(dims, kind)

    packed = call(
        lambda *refs: send_rows_kernel(experts, *refs), shape(main, features + part), 10**6
    )(ids, keep, lower_out)
    arrived = exchange(packed, experts)
    cot_packed, mix, used = call(
        lambda *refs: send_cot_kernel(experts, *refs),
        (
            shape(main, features + part + facts_width),
            shape(tokens, 4 * main),
            shape(tokens, 2 * main),
        ),
        10**6,
    )(ids, keep, lower_out, upper_cot, router)
    cot_packed, gate_up, arrived = lax.optimization_barrier((cot_packed, gate_up, arrived))
    cot_arrived = exchange(cot_packed, experts)

    row_block = unpack(arrived, features, experts)
    projected = jnp.dot(row_block, gate_up, preferred_element_type=f32)
    gate_part = projected[:, :hidden_units]
    up_part = projected[:, hidden_units:]
    gate_sig = jax.nn.sigmoid(gate_part)
    activated = gate_part * gate_sig
    hidden = (activated * up_part).astype(bf16)
    slots = main + experts
    out_packed = call(
        lambda *refs: outputs_kernel(experts, *refs),
        shape(main, features + 2 * part),
        10**6,
        grid=(fold + 2,),
        in_specs=[
            pl.BlockSpec((slots, hidden_units), lambda i: (0, 0)),
            pl.BlockSpec((hidden_units, part), lambda i: (0, jnp.minimum(i, fold - 1))),
        ],
        out_specs=pl.BlockSpec((main, part), lambda i: (0, i)),
        scratch_shapes=[pltpu.VMEM((main, part), f32)],
    )(hidden, down)

    own = lax.axis_index("expert").astype(i32).reshape(1)
    block = pl.BlockSpec((main, part), lambda i: (0, fold + 1))
    out_packed, logit_grad = call(
        lambda own, cot, rows, sent, out, grad: router_kernel(
            experts, own, cot, rows, sent, out, grad
        ),
        (shape(main, features + 2 * part), shape(2, main, 128, kind=f32)),
        10**6,
        aliases={3: 0},
        grid=(1,),
        in_specs=[
            scalar,
            whole,
            whole,
            pl.BlockSpec((main, features + 2 * part), lambda i: (0, 0)),
        ],
        out_specs=(block, pl.BlockSpec((2, main, 128), lambda i: (0, 0, 0))),
    )(own, cot_arrived, arrived, out_packed)
    out_packed, cot_arrived, hidden, row_block, logit_grad = lax.optimization_barrier(
        (out_packed, cot_arrived, hidden, row_block, logit_grad)
    )
    out_back = exchange(out_packed, experts)

    joined, grads = call(
        lambda *refs: hidden_kernel(experts, *refs),
        (shape(slots, 2 * hidden_units), shape(slots, features)),
        10**6,
    )(cot_arrived, projected, down)
    both = call(
        grads_kernel,
        shape(features, 3 * hidden_units),
        10**6,
        grid=(fold,),
        in_specs=[
            pl.BlockSpec((slots, part), lambda i: (0, i)),
            pl.BlockSpec((slots, 2 * hidden_units), lambda i: (0, 0)),
            pl.BlockSpec((slots, part), lambda i: (0, i)),
            pl.BlockSpec((slots, hidden_units), lambda i: (0, 0)),
        ],
        out_specs=pl.BlockSpec((part, 3 * hidden_units), lambda i: (i, 0)),
    )(row_block, joined, grads, hidden)
    both = lax.psum_scatter(both, "dp", scatter_dimension=0, tiled=True)
    rows_packed = call(
        lambda *refs: rows_kernel(experts, *refs),
        shape(main, features + part),
        10**6,
        grid=(fold + 1,),
        in_specs=[
            pl.BlockSpec((slots, 2 * hidden_units), lambda i: (0, 0)),
            pl.BlockSpec((part, 2 * hidden_units), lambda i: (jnp.minimum(i, fold - 1), 0)),
            pl.BlockSpec((2, main, 128), lambda i: (0, 0, 0)),
            pl.BlockSpec((experts, part), lambda i: (0, jnp.minimum(i, fold - 1))),
        ],
        out_specs=pl.BlockSpec((main, part), lambda i: (0, i)),
        scratch_shapes=[pltpu.VMEM((main, part), f32)],
    )(joined, gate_up, logit_grad, router)
    router_row = call(
        reduce_kernel,
        shape(fold, part, kind=f32),
        3 * 10**11,
        grid=(1,),
        in_specs=[pl.BlockSpec((main, part), lambda i: (0, fold + 1))],
        out_specs=pl.BlockSpec((fold, part), lambda i: (0, 0)),
    )(out_back)
    rows_packed, router_row = lax.optimization_barrier((rows_packed, router_row))
    rows_back = exchange(rows_packed, experts)
    step, copies = 1, lax.axis_size("dp")
    while step < copies:
        pairs = [(d, d ^ step) for d in range(copies)]
        router_row = router_row + lax.ppermute(router_row, "dp", pairs)
        step *= 2
    upper_input = call(upper_kernel, shape(tokens, features, kind=f32), 10**6)(
        upper_out, out_back, mix
    )
    router_all = jnp.broadcast_to(router_row, (experts, fold, part))
    router_all, both, rows_back = lax.optimization_barrier((router_all, both, rows_back))
    router_all = exchange(router_all.reshape(main, part), experts)
    router_grad = router_all.reshape(experts, features).T
    lower_grad = call(lower_kernel, shape(tokens, features, kind=f32), 10**6)(
        lower_cot, rows_back, used
    )
    return (
        upper_input,
        lower_grad,
        both[None, :, : 2 * hidden_units],
        both[None, :, 2 * hidden_units :],
        router_grad,
    )


def solution(mesh):
    blocks = P(("expert", "dp"), None)
    split = P("expert", "dp", None)
    return jax.shard_map(
        body,
        mesh=mesh,
        in_specs=(blocks, blocks, blocks, blocks, split, split, P(), blocks, blocks),
        out_specs=(blocks, blocks, split, split, P()),
        check_vma=False,
    )
```

```python
import jax
import jax.numpy as jnp
from jax import lax
from jax.experimental import pallas as pl
from jax.experimental.pallas import tpu as pltpu
from jax.sharding import PartitionSpec as P

residual_scale = 128.0 ** (-0.5)
highest = lax.Precision.HIGHEST
contract_last = (((1,), (1,)), ((), ()))
contract_first = (((0,), (0,)), ((), ()))
f32, bf16, i32 = jnp.float32, jnp.bfloat16, jnp.int32
fold = 8
facts_width = 128


def dot(left, right, dims=(((1,), (0,)), ((), ()))):
    return lax.dot_general(left, right, dims, preferred_element_type=f32)


def call(kernel, shapes, cost, aliases=None, **specs):
    return pl.pallas_call(
        kernel,
        out_shape=shapes,
        input_output_aliases=aliases or {},
        cost_estimate=pl.CostEstimate(flops=cost, bytes_accessed=0, transcendentals=0),
        compiler_params=pltpu.CompilerParams(vmem_limit_bytes=48 * 2**20),
        **specs,
    )


def places(ids, experts):
    tokens = ids.shape[1]
    rows = lax.broadcasted_iota(i32, (experts, tokens), 0)
    hot = [(rows == ids[k : k + 1, :]).astype(f32) for k in range(2)]
    earlier = lax.broadcasted_iota(i32, (tokens, tokens), 0) < lax.broadcasted_iota(
        i32, (tokens, tokens), 1
    )
    counts = dot((hot[0] + hot[1]).astype(bf16), earlier.astype(f32).astype(bf16))
    slots = []
    for k in range(2):
        rank = jnp.sum(hot[k] * counts, axis=0, keepdims=True).astype(i32)
        slots.append(
            jnp.where(rank < fold, ids[k : k + 1, :] * fold + rank, -1 - ids[k : k + 1, :])
        )
    return hot, slots


def spread(slots, values, experts):
    tokens = slots[0].shape[1]
    rows = lax.broadcasted_iota(i32, (experts * fold, tokens), 0)
    ninth = -1 - rows // fold
    zero = jnp.zeros((), f32)
    main = sum(jnp.where(rows == slots[k], values[k], zero) for k in range(2))
    extra = sum(jnp.where(ninth == slots[k], values[k], zero) for k in range(2))
    return main, extra


def gather_rows(main, extra, table, scale_main, scale_extra, out):
    count, features = main.shape[0], table.shape[1]
    part = features // fold
    own = lax.broadcasted_iota(i32, extra.shape, 0) % fold
    main = main.astype(bf16)
    total = jnp.zeros((count, part), f32)
    for c in range(fold):
        piece = table[:, c * part : (c + 1) * part]
        rows = dot(main, piece)
        if scale_main is not None:
            rows = rows * scale_main
        out[:, c * part : (c + 1) * part] = rows.astype(bf16)
        total += dot(jnp.where(own == c, extra, 0.0).astype(bf16), piece)
    if scale_extra is not None:
        total = total * scale_extra
    out[:, features : features + part] = total.astype(bf16)


def weights_kernel(gate_up, down, out):
    wide = gate_up.shape[1]
    out[:, :wide] = gate_up[...]
    out[:, wide:] = down[...].astype(f32).T.astype(bf16)


def send_rows_kernel(experts, ids, keep, table, out):
    _, slots = places(ids[...], experts)
    kept = keep[...].astype(f32)
    main, extra = spread(slots, (kept[:1], kept[1:]), experts)
    gather_rows(main, extra, table, None, None, out)


def send_cot_kernel(experts, ids, keep, lower, cot, router, out, mix, used):
    ids_now = ids[...]
    features = lower.shape[1]
    part = features // fold
    hot, slots = places(ids_now, experts)
    kept = keep[...].astype(f32)
    logits = lax.dot_general(
        router[...],
        lower[...].astype(f32),
        contract_last,
        precision=highest,
        preferred_element_type=f32,
    )
    gap = jnp.sum((hot[0] - hot[1]) * logits, axis=0, keepdims=True)
    share = jax.nn.sigmoid(gap)
    rest = 1.0 - share
    used_main, used_extra = spread(slots, (kept[:1], kept[1:]), experts)
    mix_main, mix_extra = spread(slots, (share * kept[:1], rest * kept[1:]), experts)
    weight_main = jnp.sum(mix_main, axis=1, keepdims=True) * residual_scale
    weight_extra = jnp.sum(mix_extra, axis=1, keepdims=True) * residual_scale
    gather_rows(used_main, used_extra, cot, weight_main, weight_extra, out)
    partner = spread(slots, (ids_now[1:].astype(f32), ids_now[:1].astype(f32)), experts)
    other = spread(slots, (rest, share), experts)
    lane = lax.broadcasted_iota(i32, (experts * fold, facts_width), 1)
    facts = jnp.zeros((experts * fold, facts_width), f32)
    for k in range(2):
        number = jnp.sum(partner[k], axis=1, keepdims=True)
        factor = jnp.sum(other[k], axis=1, keepdims=True)
        high = factor.astype(bf16).astype(f32)
        for place, value in enumerate((number, high, factor - high)):
            facts = jnp.where(lane == 3 * k + place, value, facts)
    out[:, features + part :] = facts.astype(bf16)
    width = experts * fold
    for k, value in enumerate((mix_main, mix_extra)):
        value = value.T
        high = value.astype(bf16)
        mix[:, 2 * k * width : (2 * k + 1) * width] = high
        mix[:, (2 * k + 1) * width : (2 * k + 2) * width] = (value - high.astype(f32)).astype(bf16)
    for k, value in enumerate((used_main, used_extra)):
        used[:, k * width : (k + 1) * width] = value.T.astype(bf16)


def signs(facts, change, own, column, experts):
    count = change.shape[0]
    col = lax.broadcasted_iota(i32, (count, experts * fold), 1) // fold
    partner = facts[:, column : column + 1].astype(i32)
    return jnp.where(col == own, change, 0.0) - jnp.where(col == partner, change, 0.0)


def router_kernel(experts, own, cot, rows, sent, out, grad):
    count = cot.shape[0]
    features = (rows.shape[1] * fold) // (fold + 1)
    part = features // fold
    total = jnp.zeros((count, 128), f32)
    for start in range(0, features, 128):
        total += cot[:, start : start + 128].astype(f32) * sent[:, start : start + 128].astype(f32)
    extra = jnp.zeros((count, 128), f32)
    for start in range(features, features + part, 128):
        extra += cot[:, start : start + 128].astype(f32) * sent[:, start : start + 128].astype(f32)
    extra = extra.reshape(experts, fold, 128)
    extra = jnp.broadcast_to(jnp.sum(extra, axis=1, keepdims=True), extra.shape)
    facts = cot[:, features + part :].astype(f32)
    changes = []
    for k, value in enumerate((total, extra.reshape(count, 128))):
        inner = jnp.sum(value, axis=1, keepdims=True)
        change = inner * (facts[:, 3 * k + 1 : 3 * k + 2] + facts[:, 3 * k + 2 : 3 * k + 3])
        changes.append(signs(facts, change, own[0], 3 * k, experts))
    row = lax.broadcasted_iota(i32, (count, count), 0) % fold
    lane = lax.broadcasted_iota(i32, (count, count), 1) % fold
    result = jnp.zeros((count, part), f32)
    for c in range(fold):
        left = jnp.where(lane == c, changes[0], 0.0).astype(bf16)
        result += dot(left, rows[:, c * part : (c + 1) * part], contract_first)
        left = jnp.where((lane == c) & (row == c), changes[1], 0.0).astype(bf16)
        result += dot(left, rows[:, features : features + part], contract_first)
    out[...] = result.astype(bf16)
    pick = lax.broadcasted_iota(i32, (count, 128), 0) == fold * lax.broadcasted_iota(
        i32, (count, 128), 1
    )
    pick = pick.astype(f32).astype(bf16)
    for k in range(2):
        high = changes[k].astype(bf16)
        low = (changes[k] - high.astype(f32)).astype(bf16)
        grad[k] = dot(high, pick) + dot(low, pick)


def upper_kernel(upper, back, mix, out):
    features = upper.shape[1]
    part = features // fold
    width = mix.shape[1] // 4
    lane = lax.broadcasted_iota(i32, (mix.shape[0], width), 1) % fold
    main_high, main_low = mix[:, :width], mix[:, width : 2 * width]
    extra_high = mix[:, 2 * width : 3 * width].astype(f32)
    extra_low = mix[:, 3 * width :].astype(f32)
    folded = back[:, features : features + part]
    for c in range(fold):
        piece = back[:, c * part : (c + 1) * part]
        mixed = dot(main_high, piece) + dot(main_low, piece)
        mixed += dot(jnp.where(lane == c, extra_high, 0.0).astype(bf16), folded)
        mixed += dot(jnp.where(lane == c, extra_low, 0.0).astype(bf16), folded)
        out[:, c * part : (c + 1) * part] = (
            upper[:, c * part : (c + 1) * part] - residual_scale * mixed
        )


def lower_kernel(lower_cot, back, used, out):
    features = lower_cot.shape[1]
    part = features // fold
    width = used.shape[1] // 2
    lane = lax.broadcasted_iota(i32, (used.shape[0], width), 1) % fold
    main, extra = used[:, :width], used[:, width:].astype(f32)
    folded = back[:, features : features + part]
    for c in range(fold):
        rows = dot(main, back[:, c * part : (c + 1) * part])
        rows += dot(jnp.where(lane == c, extra, 0.0).astype(bf16), folded)
        out[:, c * part : (c + 1) * part] = (
            lower_cot[:, c * part : (c + 1) * part].astype(f32) + rows
        )


def hidden_kernel(experts, cot, projected, down, joined, rows):
    features, units = down.shape
    part = features // fold
    main = experts * fold
    order = lax.broadcasted_iota(i32, (main, main), 1)
    place = lax.broadcasted_iota(i32, (main, main), 0)
    order = order == (place % experts) * fold + place // experts
    extra = dot(order.astype(f32).astype(bf16), cot[:, features : features + part]).astype(bf16)
    rows[:main, :] = cot[:, :features]
    for c in range(fold):
        rows[main:, c * part : (c + 1) * part] = extra[c * experts : (c + 1) * experts]
    back = dot(rows[...], down[...])
    gate, up = projected[:, :units], projected[:, units:]
    gate_sig = jax.nn.sigmoid(gate)
    activated = gate * gate_sig
    joined[:, :units] = (back * up * (gate_sig * (1.0 + gate * (1.0 - gate_sig)))).astype(bf16)
    joined[:, units:] = (back * activated).astype(bf16)


def outputs_kernel(experts, hidden, down, out):
    main = experts * fold
    features = down.shape[0]
    part = features // fold
    total = jnp.zeros((main, part), f32)
    for c in range(fold):
        result = dot(hidden[...], down[c * part : (c + 1) * part, :], contract_last)
        out[:, c * part : (c + 1) * part] = result[:main].astype(bf16)
        total += unfolded(result[main:].astype(bf16), c, experts)
    out[:, features : features + part] = total.astype(bf16)
    out[:, features + part :] = jnp.zeros((main, part), bf16)


def halves(value):
    high = value.astype(bf16)
    return high, (value - high.astype(f32)).astype(bf16)


def unfolded(extra, step, experts):
    row = lax.broadcasted_iota(i32, (experts * fold, extra.shape[0]), 0)
    lane = lax.broadcasted_iota(i32, (experts * fold, extra.shape[0]), 1) % experts
    return dot((row == lane * fold + step).astype(f32).astype(bf16), extra)


def rows_kernel(experts, joined, gate_up, grad, router, out, total):
    step = pl.program_id(0)
    main = experts * fold

    @pl.when(step == 0)
    def _():
        total[...] = jnp.zeros_like(total)

    @pl.when(step < fold)
    def _():
        result = dot(joined[...], gate_up[...], contract_last)
        left = grad[...].reshape(2 * main, grad.shape[2])[:, :experts]
        left_high, left_low = halves(left)
        right_high, right_low = halves(router[...])
        change = dot(
            jnp.concatenate([left_high, left_low, left_high], axis=1),
            jnp.concatenate([right_high, right_high, right_low], axis=0),
        )
        out[...] = (result[:main] + change[:main]).astype(bf16)
        own = lax.broadcasted_iota(i32, (main, out.shape[1]), 0) % fold == step
        extra = result[main:]
        total[...] += unfolded(jnp.concatenate(halves(extra), axis=0), step, experts)
        total[...] += jnp.where(own, change[main:], 0.0)

    @pl.when(step == fold)
    def _():
        out[...] = total[...].astype(bf16)


def reduce_kernel(back, out):
    folded = back[...].astype(f32).reshape(back.shape[0] // fold, *out.shape)
    out[...] = jnp.sum(folded, axis=0)


def order_kernel(experts, own, parts, out):
    part = parts.shape[2]
    for e in range(experts):
        piece = parts[own[0] ^ e]
        for c in range(fold):
            out[e : e + 1, c * part : (c + 1) * part] = piece[c : c + 1]


def grads_kernel(rows, joined, cot, hidden, out):
    wide = joined.shape[1]
    out[:, :wide] = dot(rows[...], joined[...], contract_first).astype(bf16)
    out[:, wide:] = dot(cot[...], hidden[...], contract_first).astype(bf16)


def exchange(array, experts):
    width = array.shape[1]
    moved = lax.all_to_all(
        array.reshape(experts, fold, width), "expert", split_axis=0, concat_axis=0, tiled=True
    )
    return moved.reshape(experts * fold, width)


def unpack(block, features, experts):
    part = features // fold
    extra = block[:, features : features + part].reshape(experts, features)
    return jnp.concatenate([block[:, :features], extra], axis=0)


def body(
    upper_out,
    lower_out,
    upper_cot,
    lower_cot,
    gate_up_weight,
    down_weight,
    router_weight,
    expert_ids,
    keep_mask,
):
    tokens, features = lower_out.shape
    experts = router_weight.shape[1]
    hidden_units = down_weight.shape[2]
    main = experts * fold
    part = features // fold
    ids, keep, router = expert_ids.T, keep_mask.T, router_weight.T
    whole = pl.BlockSpec(memory_space=pltpu.VMEM)
    scalar = pl.BlockSpec(memory_space=pltpu.SMEM)

    def shape(*dims, kind=bf16):
        return jax.ShapeDtypeStruct(dims, kind)

    weights = call(weights_kernel, shape(gate_up_weight.shape[1], 3 * hidden_units), 10**6)(
        gate_up_weight[0], down_weight[0].T
    )
    weights = lax.all_gather(weights, "dp", axis=0, tiled=True)
    gate_up, down = weights[:, : 2 * hidden_units], weights[:, 2 * hidden_units :]
    packed = call(
        lambda *refs: send_rows_kernel(experts, *refs), shape(main, features + part), 10**6
    )(ids, keep, lower_out)
    arrived = exchange(packed, experts)
    cot_packed, mix, used = call(
        lambda *refs: send_cot_kernel(experts, *refs),
        (
            shape(main, features + part + facts_width),
            shape(tokens, 4 * main),
            shape(tokens, 2 * main),
        ),
        3 * 10**11,
    )(ids, keep, lower_out, upper_cot, router)
    cot_packed, arrived = lax.optimization_barrier((cot_packed, arrived))
    cot_arrived = exchange(cot_packed, experts)

    row_block = unpack(arrived, features, experts)
    projected = jnp.dot(row_block, gate_up, preferred_element_type=f32)
    gate_part = projected[:, :hidden_units]
    up_part = projected[:, hidden_units:]
    gate_sig = jax.nn.sigmoid(gate_part)
    activated = gate_part * gate_sig
    hidden = (activated * up_part).astype(bf16)
    slots = main + experts
    out_packed = call(
        lambda *refs: outputs_kernel(experts, *refs),
        shape(main, features + 2 * part),
        10**6,
    )(hidden, down)

    own = lax.axis_index("expert").astype(i32).reshape(1)
    block = pl.BlockSpec((main, part), lambda i: (0, fold + 1))
    out_packed, logit_grad = call(
        lambda own, cot, rows, sent, out, grad: router_kernel(
            experts, own, cot, rows, sent, out, grad
        ),
        (shape(main, features + 2 * part), shape(2, main, 128, kind=f32)),
        10**6,
        aliases={3: 0},
        grid=(1,),
        in_specs=[
            scalar,
            whole,
            whole,
            pl.BlockSpec((main, features + 2 * part), lambda i: (0, 0)),
        ],
        out_specs=(block, pl.BlockSpec((2, main, 128), lambda i: (0, 0, 0))),
    )(own, cot_arrived, arrived, out_packed)
    out_packed, cot_arrived, hidden, row_block, logit_grad = lax.optimization_barrier(
        (out_packed, cot_arrived, hidden, row_block, logit_grad)
    )
    out_back = exchange(out_packed, experts)

    joined, grads = call(
        lambda *refs: hidden_kernel(experts, *refs),
        (shape(slots, 2 * hidden_units), shape(slots, features)),
        10**6,
    )(cot_arrived, projected, down)
    both = call(
        grads_kernel,
        shape(features, 3 * hidden_units),
        10**6,
        grid=(fold,),
        in_specs=[
            pl.BlockSpec((slots, part), lambda i: (0, i)),
            pl.BlockSpec((slots, 2 * hidden_units), lambda i: (0, 0)),
            pl.BlockSpec((slots, part), lambda i: (0, i)),
            pl.BlockSpec((slots, hidden_units), lambda i: (0, 0)),
        ],
        out_specs=pl.BlockSpec((part, 3 * hidden_units), lambda i: (i, 0)),
    )(row_block, joined, grads, hidden)
    both = lax.psum_scatter(both, "dp", scatter_dimension=0, tiled=True)
    rows_packed = call(
        lambda *refs: rows_kernel(experts, *refs),
        shape(main, features + part),
        10**6,
        grid=(fold + 1,),
        in_specs=[
            pl.BlockSpec((slots, 2 * hidden_units), lambda i: (0, 0)),
            pl.BlockSpec((part, 2 * hidden_units), lambda i: (jnp.minimum(i, fold - 1), 0)),
            pl.BlockSpec((2, main, 128), lambda i: (0, 0, 0)),
            pl.BlockSpec((experts, part), lambda i: (0, jnp.minimum(i, fold - 1))),
        ],
        out_specs=pl.BlockSpec((main, part), lambda i: (0, i)),
        scratch_shapes=[pltpu.VMEM((main, part), f32)],
    )(joined, weights, logit_grad, router)
    router_row = call(
        reduce_kernel,
        shape(fold, part, kind=f32),
        3 * 10**11,
        grid=(1,),
        in_specs=[pl.BlockSpec((main, part), lambda i: (0, fold + 1))],
        out_specs=pl.BlockSpec((fold, part), lambda i: (0, 0)),
    )(out_back)
    rows_packed, router_row = lax.optimization_barrier((rows_packed, router_row))
    rows_back = exchange(rows_packed, experts)
    step, copies = 1, lax.axis_size("dp")
    while step < copies:
        pairs = [(d, d ^ step) for d in range(copies)]
        router_row = router_row + lax.ppermute(router_row, "dp", pairs)
        step *= 2
    upper_input = call(upper_kernel, shape(tokens, features, kind=f32), 10**6)(
        upper_out, out_back, mix
    )
    router_all = router_row[None]
    step = 1
    while step < experts:
        pairs = [(e, e ^ step) for e in range(experts)]
        theirs = lax.ppermute(router_all, "expert", pairs)
        router_all = jnp.concatenate([router_all, theirs], axis=0)
        step *= 2
    router_grad = call(
        lambda own, parts, out: order_kernel(experts, own, parts, out),
        shape(experts, features, kind=f32),
        10**6,
        in_specs=[scalar, whole],
        out_specs=whole,
    )(own, router_all).T
    lower_grad = call(lower_kernel, shape(tokens, features, kind=f32), 10**6)(
        lower_cot, rows_back, used
    )
    return (
        upper_input,
        lower_grad,
        both[None, :, : 2 * hidden_units],
        both[None, :, 2 * hidden_units :],
        router_grad,
    )


def solution(mesh):
    blocks = P(("expert", "dp"), None)
    split = P("expert", "dp", None)
    return jax.shard_map(
        body,
        mesh=mesh,
        in_specs=(blocks, blocks, blocks, blocks, split, split, P(), blocks, blocks),
        out_specs=(blocks, blocks, split, split, P()),
        check_vma=False,
    )
```

```python
import jax
import jax.numpy as jnp
from jax import lax
from jax.experimental import pallas as pl
from jax.experimental.pallas import tpu as pltpu
from jax.sharding import PartitionSpec as P

residual_scale = 128.0 ** (-0.5)
highest = lax.Precision.HIGHEST
contract_last = (((1,), (1,)), ((), ()))
contract_first = (((0,), (0,)), ((), ()))
f32, bf16, i32 = jnp.float32, jnp.bfloat16, jnp.int32
fold = 8
facts_width = 128


def dot(left, right, dims=(((1,), (0,)), ((), ()))):
    return lax.dot_general(left, right, dims, preferred_element_type=f32)


def call(kernel, shapes, cost, aliases=None, **specs):
    return pl.pallas_call(
        kernel,
        out_shape=shapes,
        input_output_aliases=aliases or {},
        cost_estimate=pl.CostEstimate(flops=cost, bytes_accessed=0, transcendentals=0),
        compiler_params=pltpu.CompilerParams(vmem_limit_bytes=48 * 2**20),
        **specs,
    )


def places(ids, experts):
    tokens = ids.shape[1]
    rows = lax.broadcasted_iota(i32, (experts, tokens), 0)
    hot = [(rows == ids[k : k + 1, :]).astype(f32) for k in range(2)]
    earlier = lax.broadcasted_iota(i32, (tokens, tokens), 0) < lax.broadcasted_iota(
        i32, (tokens, tokens), 1
    )
    counts = dot((hot[0] + hot[1]).astype(bf16), earlier.astype(f32).astype(bf16))
    slots = []
    for k in range(2):
        rank = jnp.sum(hot[k] * counts, axis=0, keepdims=True).astype(i32)
        slots.append(
            jnp.where(rank < fold, ids[k : k + 1, :] * fold + rank, -1 - ids[k : k + 1, :])
        )
    return hot, slots


def spread(slots, values, experts):
    tokens = slots[0].shape[1]
    rows = lax.broadcasted_iota(i32, (experts * fold, tokens), 0)
    ninth = -1 - rows // fold
    zero = jnp.zeros((), f32)
    main = sum(jnp.where(rows == slots[k], values[k], zero) for k in range(2))
    extra = sum(jnp.where(ninth == slots[k], values[k], zero) for k in range(2))
    return main, extra


def gather_rows(main, extra, table, scale_main, scale_extra, out):
    count, features = main.shape[0], table.shape[1]
    part = features // fold
    own = lax.broadcasted_iota(i32, extra.shape, 0) % fold
    main = main.astype(bf16)
    total = jnp.zeros((count, part), f32)
    for c in range(fold):
        piece = table[:, c * part : (c + 1) * part]
        rows = dot(main, piece)
        if scale_main is not None:
            rows = rows * scale_main
        out[:, c * part : (c + 1) * part] = rows.astype(bf16)
        total += dot(jnp.where(own == c, extra, 0.0).astype(bf16), piece)
    if scale_extra is not None:
        total = total * scale_extra
    out[:, features : features + part] = total.astype(bf16)


def send_rows_kernel(experts, ids, keep, table, gate_up, down, weights, out):
    wide = gate_up.shape[1]
    weights[:, :wide] = gate_up[...]
    weights[:, wide:] = down[...].astype(f32).T.astype(bf16)
    _, slots = places(ids[...], experts)
    kept = keep[...].astype(f32)
    main, extra = spread(slots, (kept[:1], kept[1:]), experts)
    gather_rows(main, extra, table, None, None, out)


def send_cot_kernel(experts, ids, keep, lower, cot, router, out, mix, used):
    ids_now = ids[...]
    features = lower.shape[1]
    part = features // fold
    hot, slots = places(ids_now, experts)
    kept = keep[...].astype(f32)
    logits = lax.dot_general(
        router[...],
        lower[...].astype(f32),
        contract_last,
        precision=highest,
        preferred_element_type=f32,
    )
    gap = jnp.sum((hot[0] - hot[1]) * logits, axis=0, keepdims=True)
    share = jax.nn.sigmoid(gap)
    rest = 1.0 - share
    used_main, used_extra = spread(slots, (kept[:1], kept[1:]), experts)
    mix_main, mix_extra = spread(slots, (share * kept[:1], rest * kept[1:]), experts)
    weight_main = jnp.sum(mix_main, axis=1, keepdims=True) * residual_scale
    weight_extra = jnp.sum(mix_extra, axis=1, keepdims=True) * residual_scale
    gather_rows(used_main, used_extra, cot, weight_main, weight_extra, out)
    partner = spread(slots, (ids_now[1:].astype(f32), ids_now[:1].astype(f32)), experts)
    other = spread(slots, (rest, share), experts)
    lane = lax.broadcasted_iota(i32, (experts * fold, facts_width), 1)
    facts = jnp.zeros((experts * fold, facts_width), f32)
    for k in range(2):
        number = jnp.sum(partner[k], axis=1, keepdims=True)
        factor = jnp.sum(other[k], axis=1, keepdims=True)
        high = factor.astype(bf16).astype(f32)
        for place, value in enumerate((number, high, factor - high)):
            facts = jnp.where(lane == 3 * k + place, value, facts)
    out[:, features + part :] = facts.astype(bf16)
    width = experts * fold
    for k, value in enumerate((mix_main, mix_extra)):
        value = value.T
        high = value.astype(bf16)
        mix[:, 2 * k * width : (2 * k + 1) * width] = high
        mix[:, (2 * k + 1) * width : (2 * k + 2) * width] = (value - high.astype(f32)).astype(bf16)
    for k, value in enumerate((used_main, used_extra)):
        used[:, k * width : (k + 1) * width] = value.T.astype(bf16)


def reverse(number, experts):
    result, bits = number * 0, experts.bit_length() - 1
    for bit in range(bits):
        result = result | (((number >> bit) & 1) << (bits - 1 - bit))
    return result


def router_kernel(experts, own, cot, rows, sent, out, grad):
    count = cot.shape[0]
    features = (rows.shape[1] * fold) // (fold + 1)
    part = features // fold
    total = jnp.zeros((count, 128), f32)
    for start in range(0, features, 128):
        total += cot[:, start : start + 128].astype(f32) * sent[:, start : start + 128].astype(f32)
    extra = jnp.zeros((count, 128), f32)
    for start in range(features, features + part, 128):
        extra += cot[:, start : start + 128].astype(f32) * sent[:, start : start + 128].astype(f32)
    extra = extra.reshape(experts, fold, 128)
    extra = jnp.broadcast_to(jnp.sum(extra, axis=1, keepdims=True), extra.shape)
    facts = cot[:, features + part :].astype(f32)
    me = own[0]
    column = lax.broadcasted_iota(i32, (count, 128), 1)
    lane = lax.broadcasted_iota(i32, (count, count), 1)
    row = lax.broadcasted_iota(i32, (count, count), 0) % fold
    lefts = []
    for k, value in enumerate((total, extra.reshape(count, 128))):
        inner = jnp.sum(value, axis=1, keepdims=True)
        change = inner * (facts[:, 3 * k + 1 : 3 * k + 2] + facts[:, 3 * k + 2 : 3 * k + 3])
        partner = facts[:, 3 * k : 3 * k + 1].astype(i32)
        grad[k] = jnp.where(column == me, change, 0.0) - jnp.where(column == partner, change, 0.0)
        away = reverse(partner ^ me, experts)
        at = column if k == 0 else lane % experts
        left = jnp.where(at == 0, change, 0.0) - jnp.where(at == away, change, 0.0)
        if k == 1:
            left = jnp.where(lane // experts == row, left, 0.0)
        lefts.append(left.astype(bf16))
    ninth = dot(lefts[1], rows[:, features:], contract_first)
    for c in range(fold):
        piece = dot(lefts[0], rows[:, c * part : (c + 1) * part], contract_first)
        out[:, c, :] = piece[:experts] + ninth[c * experts : (c + 1) * experts]


def upper_kernel(upper, back, mix, out):
    features = upper.shape[1]
    part = features // fold
    width = mix.shape[1] // 4
    lane = lax.broadcasted_iota(i32, (mix.shape[0], width), 1) % fold
    main_high, main_low = mix[:, :width], mix[:, width : 2 * width]
    extra_high = mix[:, 2 * width : 3 * width].astype(f32)
    extra_low = mix[:, 3 * width :].astype(f32)
    folded = back[:, features : features + part]
    for c in range(fold):
        piece = back[:, c * part : (c + 1) * part]
        mixed = dot(main_high, piece) + dot(main_low, piece)
        mixed += dot(jnp.where(lane == c, extra_high, 0.0).astype(bf16), folded)
        mixed += dot(jnp.where(lane == c, extra_low, 0.0).astype(bf16), folded)
        out[:, c * part : (c + 1) * part] = (
            upper[:, c * part : (c + 1) * part] - residual_scale * mixed
        )


def lower_kernel(lower_cot, back, used, out):
    features = lower_cot.shape[1]
    part = features // fold
    width = used.shape[1] // 2
    lane = lax.broadcasted_iota(i32, (used.shape[0], width), 1) % fold
    main, extra = used[:, :width], used[:, width:].astype(f32)
    folded = back[:, features : features + part]
    for c in range(fold):
        rows = dot(main, back[:, c * part : (c + 1) * part])
        rows += dot(jnp.where(lane == c, extra, 0.0).astype(bf16), folded)
        out[:, c * part : (c + 1) * part] = (
            lower_cot[:, c * part : (c + 1) * part].astype(f32) + rows
        )


def hidden_kernel(experts, cot, projected, down, joined, rows):
    features, units = down.shape
    part = features // fold
    main = experts * fold
    order = lax.broadcasted_iota(i32, (main, main), 1)
    place = lax.broadcasted_iota(i32, (main, main), 0)
    order = order == (place % experts) * fold + place // experts
    extra = dot(order.astype(f32).astype(bf16), cot[:, features : features + part]).astype(bf16)
    rows[:main, :] = cot[:, :features]
    for c in range(fold):
        rows[main:, c * part : (c + 1) * part] = extra[c * experts : (c + 1) * experts]
    back = dot(rows[...], down[...])
    gate, up = projected[:, :units], projected[:, units:]
    gate_sig = jax.nn.sigmoid(gate)
    activated = gate * gate_sig
    joined[:, :units] = (back * up * (gate_sig * (1.0 + gate * (1.0 - gate_sig)))).astype(bf16)
    joined[:, units:] = (back * activated).astype(bf16)


def outputs_kernel(experts, hidden, down, out):
    main = experts * fold
    features = down.shape[0]
    part = features // fold
    total = jnp.zeros((main, part), f32)
    for c in range(fold):
        result = dot(hidden[...], down[c * part : (c + 1) * part, :], contract_last)
        out[:, c * part : (c + 1) * part] = result[:main].astype(bf16)
        total += unfolded(result[main:].astype(bf16), c, experts)
    out[:, features:] = total.astype(bf16)


def halves(value):
    high = value.astype(bf16)
    return high, (value - high.astype(f32)).astype(bf16)


def unfolded(extra, step, experts):
    row = lax.broadcasted_iota(i32, (experts * fold, extra.shape[0]), 0)
    lane = lax.broadcasted_iota(i32, (experts * fold, extra.shape[0]), 1) % experts
    return dot((row == lane * fold + step).astype(f32).astype(bf16), extra)


def rows_kernel(experts, joined, gate_up, grad, router, out, total, left):
    step = pl.program_id(0)
    main = experts * fold

    @pl.when(step == 0)
    def _():
        total[...] = jnp.zeros_like(total)
        high, low = halves(grad[...].reshape(2 * main, grad.shape[2])[:, :experts])
        left[...] = jnp.concatenate([high, low, high], axis=1)

    @pl.when(step < fold)
    def _():
        result = dot(joined[...], gate_up[...], contract_last)
        high, low = halves(router[...])
        change = dot(left[...], jnp.concatenate([high, high, low], axis=0))
        out[...] = (result[:main] + change[:main]).astype(bf16)
        own = lax.broadcasted_iota(i32, (main, out.shape[1]), 0) % fold == step
        extra = unfolded(jnp.concatenate(halves(result[main:]), axis=0), step, experts)
        total[...] = jnp.where(own, extra + change[main:], total[...])

    @pl.when(step == fold)
    def _():
        out[...] = total[...].astype(bf16)


def add_kernel(*refs):
    *parts, out = refs
    out[...] = sum([ref[...] for ref in parts[1:]], parts[0][...])


def split_kernel(both, gate_up, down):
    wide = gate_up.shape[1]
    gate_up[...] = both[:, :wide]
    down[...] = both[:, wide:].astype(f32).T.astype(bf16)


def order_kernel(experts, own, parts, out):
    part = parts.shape[2]
    for e in range(experts):
        piece = parts[reverse(own[0] ^ e, experts)]
        for c in range(fold):
            out[e : e + 1, c * part : (c + 1) * part] = piece[c : c + 1]


def grads_kernel(rows, joined, cot, hidden, out):
    wide = joined.shape[1]
    out[:, :wide] = dot(rows[...], joined[...], contract_first).astype(bf16)
    out[:, wide:] = dot(cot[...], hidden[...], contract_first).astype(bf16)


def exchange(array, experts):
    width = array.shape[1]
    moved = lax.all_to_all(
        array.reshape(experts, fold, width), "expert", split_axis=0, concat_axis=0, tiled=True
    )
    return moved.reshape(experts * fold, width)


def rounds(size):
    result, bit = [], 1
    while bit < size:
        if 2 * bit < size:
            result.append((2 * bit, bit, 3 * bit))
            bit *= 4
        else:
            result.append((bit,))
            bit *= 2
    return result


def swap(array, axis, flip):
    return lax.ppermute(array, axis, [(i, i ^ flip) for i in range(lax.axis_size(axis))])


def unpack(block, features, experts):
    part = features // fold
    extra = block[:, features : features + part].reshape(experts, features)
    return jnp.concatenate([block[:, :features], extra], axis=0)


def body(
    upper_out,
    lower_out,
    upper_cot,
    lower_cot,
    gate_up_weight,
    down_weight,
    router_weight,
    expert_ids,
    keep_mask,
):
    tokens, features = lower_out.shape
    experts = router_weight.shape[1]
    hidden_units = down_weight.shape[2]
    main = experts * fold
    part = features // fold
    ids, keep, router = expert_ids.T, keep_mask.T, router_weight.T
    whole = pl.BlockSpec(memory_space=pltpu.VMEM)
    scalar = pl.BlockSpec(memory_space=pltpu.SMEM)

    def shape(*dims, kind=bf16):
        return jax.ShapeDtypeStruct(dims, kind)

    weights, packed = call(
        lambda *refs: send_rows_kernel(experts, *refs),
        (
            shape(gate_up_weight.shape[1], 3 * hidden_units),
            shape(main, features + part),
        ),
        10**6,
    )(ids, keep, lower_out, gate_up_weight[0], down_weight[0].T)
    weights = lax.all_gather(weights, "dp", axis=0, tiled=True)
    gate_up, down = weights[:, : 2 * hidden_units], weights[:, 2 * hidden_units :]
    arrived = exchange(packed, experts)
    cot_packed, mix, used = call(
        lambda *refs: send_cot_kernel(experts, *refs),
        (
            shape(main, features + part + facts_width),
            shape(tokens, 4 * main),
            shape(tokens, 2 * main),
        ),
        3 * 10**11,
    )(ids, keep, lower_out, upper_cot, router)
    cot_packed, arrived = lax.optimization_barrier((cot_packed, arrived))
    cot_arrived = exchange(cot_packed, experts)

    row_block = unpack(arrived, features, experts)
    projected = jnp.dot(row_block, gate_up, preferred_element_type=f32)
    gate_part = projected[:, :hidden_units]
    up_part = projected[:, hidden_units:]
    gate_sig = jax.nn.sigmoid(gate_part)
    activated = gate_part * gate_sig
    hidden = (activated * up_part).astype(bf16)
    slots = main + experts
    out_packed = call(
        lambda *refs: outputs_kernel(experts, *refs),
        shape(main, features + part),
        10**6,
    )(hidden, down)

    own = lax.axis_index("expert").astype(i32).reshape(1)
    out_back = exchange(out_packed, experts)
    joined, grads = call(
        lambda *refs: hidden_kernel(experts, *refs),
        (shape(slots, 2 * hidden_units), shape(slots, features)),
        10**6,
    )(cot_arrived, projected, down)
    both = call(
        grads_kernel,
        shape(features, 3 * hidden_units),
        10**6,
        grid=(fold,),
        in_specs=[
            pl.BlockSpec((slots, part), lambda i: (0, i)),
            pl.BlockSpec((slots, 2 * hidden_units), lambda i: (0, 0)),
            pl.BlockSpec((slots, part), lambda i: (0, i)),
            pl.BlockSpec((slots, hidden_units), lambda i: (0, 0)),
        ],
        out_specs=pl.BlockSpec((part, 3 * hidden_units), lambda i: (i, 0)),
    )(row_block, joined, grads, hidden)
    both, cot_arrived = lax.optimization_barrier((both, cot_arrived))
    router_part, logit_grad = call(
        lambda *refs: router_kernel(experts, *refs),
        (shape(experts, fold, part, kind=f32), shape(2, main, 128, kind=f32)),
        10**6,
        in_specs=[scalar, whole, whole, whole],
        out_specs=(whole, whole),
    )(own, cot_arrived, arrived, out_packed)
    both = lax.psum_scatter(both, "dp", scatter_dimension=0, tiled=True)
    rows_packed = call(
        lambda *refs: rows_kernel(experts, *refs),
        shape(main, features + part),
        10**6,
        grid=(fold + 1,),
        in_specs=[
            pl.BlockSpec((slots, 2 * hidden_units), lambda i: (0, 0)),
            pl.BlockSpec((part, 2 * hidden_units), lambda i: (jnp.minimum(i, fold - 1), 0)),
            pl.BlockSpec((2, main, 128), lambda i: (0, 0, 0)),
            pl.BlockSpec((experts, part), lambda i: (0, jnp.minimum(i, fold - 1))),
        ],
        out_specs=pl.BlockSpec((main, part), lambda i: (0, i)),
        scratch_shapes=[
            pltpu.VMEM((main, part), f32),
            pltpu.VMEM((2 * main, 3 * experts), bf16),
        ],
    )(joined, weights, logit_grad, router)
    for count, flips in enumerate(rounds(experts)):
        piece = router_part.shape[0] // (len(flips) + 1)
        parts = [router_part[:piece]]
        for place, flip in enumerate(flips, 1):
            parts.append(swap(router_part[place * piece : (place + 1) * piece], "expert", flip))
        if count == 0:
            *parts, out_back = lax.optimization_barrier((*parts, out_back))
            router_part = call(add_kernel, shape(piece, fold, part, kind=f32), 149500 * 10**6)(*parts)
            rows_packed, router_part = lax.optimization_barrier((rows_packed, router_part))
            rows_back = exchange(rows_packed, experts)
        else:
            router_part = sum(parts[1:], parts[0])
    copies = lax.axis_size("dp")
    flips = [1] + [flip for flip in range(2, copies, 2)]
    router_part = router_part + (swap(router_part, "dp", 1) if copies > 1 else 0.0)
    parts = [swap(router_part, "dp", flip) for flip in flips[1:]]
    router_all = sum(parts, router_part)
    upper_input = call(upper_kernel, shape(tokens, features, kind=f32), 10**6)(
        upper_out, out_back, mix
    )
    for flips in reversed(rounds(experts)):
        parts = [swap(router_all, "expert", flip) for flip in flips]
        router_all = jnp.concatenate([router_all, *parts], axis=0)
    router_grad = call(
        lambda own, parts, out: order_kernel(experts, own, parts, out),
        shape(experts, features, kind=f32),
        10**6,
        in_specs=[scalar, whole],
        out_specs=whole,
    )(own, router_all).T
    lower_grad = call(lower_kernel, shape(tokens, features, kind=f32), 10**6)(
        lower_cot, rows_back, used
    )
    lower_grad, both = lax.optimization_barrier((lower_grad, both))
    gate_up_grad, down_grad = call(
        split_kernel,
        (shape(both.shape[0], 2 * hidden_units), shape(hidden_units, both.shape[0])),
        10**6,
    )(both)
    return upper_input, lower_grad, gate_up_grad[None], down_grad.T[None], router_grad


def solution(mesh):
    blocks = P(("expert", "dp"), None)
    split = P("expert", "dp", None)
    return jax.shard_map(
        body,
        mesh=mesh,
        in_specs=(blocks, blocks, blocks, blocks, split, split, P(), blocks, blocks),
        out_specs=(blocks, blocks, split, split, P()),
        check_vma=False,
    )
```

```python
import jax
import jax.numpy as jnp
from jax import lax
from jax.experimental import pallas as pl
from jax.experimental.pallas import tpu as pltpu
from jax.sharding import PartitionSpec as P

residual_scale = 128.0 ** (-0.5)
highest = lax.Precision.HIGHEST
contract_last = (((1,), (1,)), ((), ()))
contract_first = (((0,), (0,)), ((), ()))
f32, bf16, i32 = jnp.float32, jnp.bfloat16, jnp.int32
fold = 8
facts_width = 128


def dot(left, right, dims=(((1,), (0,)), ((), ()))):
    return lax.dot_general(left, right, dims, preferred_element_type=f32)


def call(kernel, shapes, cost, aliases=None, **specs):
    return pl.pallas_call(
        kernel,
        out_shape=shapes,
        input_output_aliases=aliases or {},
        cost_estimate=pl.CostEstimate(flops=cost, bytes_accessed=0, transcendentals=0),
        compiler_params=pltpu.CompilerParams(vmem_limit_bytes=48 * 2**20),
        **specs,
    )


def places(ids, experts):
    tokens = ids.shape[1]
    rows = lax.broadcasted_iota(i32, (experts, tokens), 0)
    hot = [(rows == ids[k : k + 1, :]).astype(f32) for k in range(2)]
    earlier = lax.broadcasted_iota(i32, (tokens, tokens), 0) < lax.broadcasted_iota(
        i32, (tokens, tokens), 1
    )
    counts = dot((hot[0] + hot[1]).astype(bf16), earlier.astype(f32).astype(bf16))
    slots = []
    for k in range(2):
        rank = jnp.sum(hot[k] * counts, axis=0, keepdims=True).astype(i32)
        slots.append(
            jnp.where(rank < fold, ids[k : k + 1, :] * fold + rank, -1 - ids[k : k + 1, :])
        )
    return hot, slots


def spread(slots, values, experts):
    tokens = slots[0].shape[1]
    rows = lax.broadcasted_iota(i32, (experts * fold, tokens), 0)
    ninth = -1 - rows // fold
    zero = jnp.zeros((), f32)
    main = sum(jnp.where(rows == slots[k], values[k], zero) for k in range(2))
    extra = sum(jnp.where(ninth == slots[k], values[k], zero) for k in range(2))
    return main, extra


def gather_rows(main, extra, table, scale_main, scale_extra, out):
    count, features = main.shape[0], table.shape[1]
    part = features // fold
    own = lax.broadcasted_iota(i32, extra.shape, 0) % fold
    main = main.astype(bf16)
    total = jnp.zeros((count, part), f32)
    for c in range(fold):
        piece = table[:, c * part : (c + 1) * part]
        rows = dot(main, piece)
        if scale_main is not None:
            rows = rows * scale_main
        out[:, c * part : (c + 1) * part] = rows.astype(bf16)
        total += dot(jnp.where(own == c, extra, 0.0).astype(bf16), piece)
    if scale_extra is not None:
        total = total * scale_extra
    out[:, features : features + part] = total.astype(bf16)


def send_rows_kernel(experts, ids, keep, table, gate_up, down, weights, out):
    wide = gate_up.shape[1]
    weights[:, :wide] = gate_up[...]
    weights[:, wide:] = down[...].astype(f32).T.astype(bf16)
    _, slots = places(ids[...], experts)
    kept = keep[...].astype(f32)
    main, extra = spread(slots, (kept[:1], kept[1:]), experts)
    gather_rows(main, extra, table, None, None, out)


def send_cot_kernel(experts, ids, keep, lower, cot, router, out, mix, used):
    ids_now = ids[...]
    features = lower.shape[1]
    part = features // fold
    hot, slots = places(ids_now, experts)
    kept = keep[...].astype(f32)
    logits = lax.dot_general(
        router[...],
        lower[...].astype(f32),
        contract_last,
        precision=highest,
        preferred_element_type=f32,
    )
    gap = jnp.sum((hot[0] - hot[1]) * logits, axis=0, keepdims=True)
    share = jax.nn.sigmoid(gap)
    rest = 1.0 - share
    used_main, used_extra = spread(slots, (kept[:1], kept[1:]), experts)
    mix_main, mix_extra = spread(slots, (share * kept[:1], rest * kept[1:]), experts)
    weight_main = jnp.sum(mix_main, axis=1, keepdims=True) * residual_scale
    weight_extra = jnp.sum(mix_extra, axis=1, keepdims=True) * residual_scale
    gather_rows(used_main, used_extra, cot, weight_main, weight_extra, out)
    partner = spread(slots, (ids_now[1:].astype(f32), ids_now[:1].astype(f32)), experts)
    other = spread(slots, (rest, share), experts)
    lane = lax.broadcasted_iota(i32, (experts * fold, facts_width), 1)
    facts = jnp.zeros((experts * fold, facts_width), f32)
    for k in range(2):
        number = jnp.sum(partner[k], axis=1, keepdims=True)
        factor = jnp.sum(other[k], axis=1, keepdims=True)
        high = factor.astype(bf16).astype(f32)
        for place, value in enumerate((number, high, factor - high)):
            facts = jnp.where(lane == 3 * k + place, value, facts)
    out[:, features + part :] = facts.astype(bf16)
    width = experts * fold
    for k, value in enumerate((mix_main, mix_extra)):
        value = value.T
        high = value.astype(bf16)
        mix[:, 2 * k * width : (2 * k + 1) * width] = high
        mix[:, (2 * k + 1) * width : (2 * k + 2) * width] = (value - high.astype(f32)).astype(bf16)
    for k, value in enumerate((used_main, used_extra)):
        used[:, k * width : (k + 1) * width] = value.T.astype(bf16)


def router_kernel(experts, own, cot, rows, sent, out, grad, total):
    count = cot.shape[0]
    features = (rows.shape[1] * fold) // (fold + 1)
    part = features // fold
    sums = jnp.zeros((count, 128), f32)
    for start in range(0, features, 128):
        sums += cot[:, start : start + 128].astype(f32) * sent[:, start : start + 128].astype(f32)
    extra = jnp.zeros((count, 128), f32)
    for start in range(features, features + part, 128):
        extra += cot[:, start : start + 128].astype(f32) * sent[:, start : start + 128].astype(f32)
    extra = extra.reshape(experts, fold, 128)
    extra = jnp.broadcast_to(jnp.sum(extra, axis=1, keepdims=True), extra.shape)
    facts = cot[:, features + part :].astype(f32)
    me = own[0]
    column = lax.broadcasted_iota(i32, (count, 128), 1)
    lane = lax.broadcasted_iota(i32, (count, count), 1)
    row = lax.broadcasted_iota(i32, (count, count), 0) % fold
    lefts = []
    for k, value in enumerate((sums, extra.reshape(count, 128))):
        inner = jnp.sum(value, axis=1, keepdims=True)
        change = inner * (facts[:, 3 * k + 1 : 3 * k + 2] + facts[:, 3 * k + 2 : 3 * k + 3])
        partner = facts[:, 3 * k : 3 * k + 1].astype(i32)
        signed = jnp.where(column == me, change, 0.0) - jnp.where(column == partner, change, 0.0)
        grad[k] = signed
        if k == 1:
            at = lane % experts
            signed = jnp.where(at == me, change, 0.0) - jnp.where(at == partner, change, 0.0)
            signed = jnp.where(lane // experts == row, signed, 0.0)
        lefts.append(signed.astype(bf16))
    ninth = dot(lefts[1], rows[:, features:], contract_first)
    for c in range(fold):
        piece = dot(lefts[0], rows[:, c * part : (c + 1) * part], contract_first)
        total[:, c, :] = piece[:experts] + ninth[c * experts : (c + 1) * experts]
    out[...] = total[...].reshape(out.shape).astype(bf16)


def upper_kernel(upper, back, mix, out):
    features = upper.shape[1]
    part = features // fold
    width = mix.shape[1] // 4
    lane = lax.broadcasted_iota(i32, (mix.shape[0], width), 1) % fold
    main_high, main_low = mix[:, :width], mix[:, width : 2 * width]
    extra_high = mix[:, 2 * width : 3 * width].astype(f32)
    extra_low = mix[:, 3 * width :].astype(f32)
    folded = back[:, features : features + part]
    for c in range(fold):
        piece = back[:, c * part : (c + 1) * part]
        mixed = dot(main_high, piece) + dot(main_low, piece)
        mixed += dot(jnp.where(lane == c, extra_high, 0.0).astype(bf16), folded)
        mixed += dot(jnp.where(lane == c, extra_low, 0.0).astype(bf16), folded)
        out[:, c * part : (c + 1) * part] = (
            upper[:, c * part : (c + 1) * part] - residual_scale * mixed
        )


def lower_kernel(lower_cot, back, used, out):
    features = lower_cot.shape[1]
    part = features // fold
    width = used.shape[1] // 2
    lane = lax.broadcasted_iota(i32, (used.shape[0], width), 1) % fold
    main, extra = used[:, :width], used[:, width:].astype(f32)
    folded = back[:, features : features + part]
    for c in range(fold):
        rows = dot(main, back[:, c * part : (c + 1) * part])
        rows += dot(jnp.where(lane == c, extra, 0.0).astype(bf16), folded)
        out[:, c * part : (c + 1) * part] = (
            lower_cot[:, c * part : (c + 1) * part].astype(f32) + rows
        )


def unpack(packed, rows, experts):
    features = rows.shape[1]
    part = features // fold
    main = experts * fold
    place = lax.broadcasted_iota(i32, (main, main), 0)
    order = lax.broadcasted_iota(i32, (main, main), 1)
    order = order == (place % experts) * fold + place // experts
    extra = dot(order.astype(f32).astype(bf16), packed[:, features : features + part]).astype(bf16)
    rows[:main, :] = packed[:, :features]
    for c in range(fold):
        rows[main:, c * part : (c + 1) * part] = extra[c * experts : (c + 1) * experts]


def hidden_kernel(experts, cot, projected, down, joined, rows):
    units = down.shape[1]
    unpack(cot, rows, experts)
    back = dot(rows[...], down[...])
    gate, up = projected[:, :units], projected[:, units:]
    gate_sig = jax.nn.sigmoid(gate)
    activated = gate * gate_sig
    joined[:, :units] = (back * up * (gate_sig * (1.0 + gate * (1.0 - gate_sig)))).astype(bf16)
    joined[:, units:] = (back * activated).astype(bf16)


def outputs_kernel(experts, hidden, down, out):
    main = experts * fold
    features = down.shape[0]
    part = features // fold
    total = jnp.zeros((main, part), f32)
    for c in range(fold):
        result = dot(hidden[...], down[c * part : (c + 1) * part, :], contract_last)
        out[:, c * part : (c + 1) * part] = result[:main].astype(bf16)
        total += unfolded(result[main:].astype(bf16), c, experts)
    out[:, features : features + part] = total.astype(bf16)
    out[:, features + part :] = jnp.zeros((main, part), bf16)


def halves(value):
    high = value.astype(bf16)
    return high, (value - high.astype(f32)).astype(bf16)


def unfolded(extra, step, experts):
    row = lax.broadcasted_iota(i32, (experts * fold, extra.shape[0]), 0)
    lane = lax.broadcasted_iota(i32, (experts * fold, extra.shape[0]), 1) % experts
    return dot((row == lane * fold + step).astype(f32).astype(bf16), extra)


def rows_kernel(experts, joined, gate_up, grad, router, out, total, left):
    step = pl.program_id(0)
    main = experts * fold

    @pl.when(step == 0)
    def _():
        total[...] = jnp.zeros_like(total)
        high, low = halves(grad[...].reshape(2 * main, grad.shape[2])[:, :experts])
        left[...] = jnp.concatenate([high, low, high], axis=1)

    @pl.when(step < fold)
    def _():
        result = dot(joined[...], gate_up[...], contract_last)
        high, low = halves(router[...])
        change = dot(left[...], jnp.concatenate([high, high, low], axis=0))
        out[...] = (result[:main] + change[:main]).astype(bf16)
        own = lax.broadcasted_iota(i32, (main, out.shape[1]), 0) % fold == step
        extra = unfolded(jnp.concatenate(halves(result[main:]), axis=0), step, experts)
        total[...] = jnp.where(own, extra + change[main:], total[...])

    @pl.when(step == fold)
    def _():
        out[...] = total[...].astype(bf16)


def reduce_kernel(back, out):
    folded = back[...].astype(f32).reshape(back.shape[0] // fold, *out.shape)
    out[...] = jnp.sum(folded, axis=0)


def split_kernel(both, gate_up, down):
    wide = gate_up.shape[1]
    gate_up[...] = both[:, :wide]
    down[...] = both[:, wide:].astype(f32).T.astype(bf16)


def order_kernel(experts, own, parts, out):
    part = parts.shape[2]
    for e in range(experts):
        piece = parts[own[0] ^ e]
        for c in range(fold):
            out[e : e + 1, c * part : (c + 1) * part] = piece[c : c + 1]


def grads_kernel(rows, joined, cot, hidden, out):
    wide = joined.shape[1]
    out[:, :wide] = dot(rows[...], joined[...], contract_first).astype(bf16)
    out[:, wide:] = dot(cot[...], hidden[...], contract_first).astype(bf16)


def exchange(array, experts):
    width = array.shape[1]
    moved = lax.all_to_all(
        array.reshape(experts, fold, width), "expert", split_axis=0, concat_axis=0, tiled=True
    )
    return moved.reshape(experts * fold, width)


def rounds(size):
    result, bit = [], 1
    while bit < size:
        if 2 * bit < size:
            result.append((bit, 2 * bit, 3 * bit))
            bit *= 4
        else:
            result.append((bit,))
            bit *= 2
    return result


def swap(array, axis, flip):
    return lax.ppermute(array, axis, [(i, i ^ flip) for i in range(lax.axis_size(axis))])


def body(
    upper_out,
    lower_out,
    upper_cot,
    lower_cot,
    gate_up_weight,
    down_weight,
    router_weight,
    expert_ids,
    keep_mask,
):
    tokens, features = lower_out.shape
    experts = router_weight.shape[1]
    hidden_units = down_weight.shape[2]
    main = experts * fold
    part = features // fold
    ids, keep, router = expert_ids.T, keep_mask.T, router_weight.T
    whole = pl.BlockSpec(memory_space=pltpu.VMEM)
    scalar = pl.BlockSpec(memory_space=pltpu.SMEM)

    def shape(*dims, kind=bf16):
        return jax.ShapeDtypeStruct(dims, kind)

    first = (ids, keep, lower_out, gate_up_weight[0], down_weight[0].T)
    shapes = (
        shape(gate_up_weight.shape[1], 3 * hidden_units),
        shape(main, features + part),
    )
    weights, packed = call(
        lambda *refs: send_rows_kernel(experts, *refs),
        shapes,
        10**6,
        grid=(1,),
        in_specs=[pl.BlockSpec(array.shape, lambda i: (0, 0)) for array in first],
        out_specs=[pl.BlockSpec(array.shape, lambda i: (0, 0)) for array in shapes],
    )(*first)
    weights = lax.all_gather(weights, "dp", axis=0, tiled=True)
    gate_up, down = weights[:, : 2 * hidden_units], weights[:, 2 * hidden_units :]
    arrived = exchange(packed, experts)
    cot_packed, mix, used = call(
        lambda *refs: send_cot_kernel(experts, *refs),
        (
            shape(main, features + part + facts_width),
            shape(tokens, 4 * main),
            shape(tokens, 2 * main),
        ),
        3 * 10**11,
    )(ids, keep, lower_out, upper_cot, router)
    cot_packed, arrived = lax.optimization_barrier((cot_packed, arrived))
    cot_arrived = exchange(cot_packed, experts)

    row_block = call(
        lambda packed, rows: unpack(packed, rows, experts), shape(main + experts, features), 10**6
    )(arrived)
    projected = jnp.dot(row_block, gate_up, preferred_element_type=f32)
    gate_part = projected[:, :hidden_units]
    up_part = projected[:, hidden_units:]
    gate_sig = jax.nn.sigmoid(gate_part)
    activated = gate_part * gate_sig
    hidden = (activated * up_part).astype(bf16)
    slots = main + experts
    out_packed = call(
        lambda *refs: outputs_kernel(experts, *refs),
        shape(main, features + 2 * part),
        10**6,
    )(hidden, down)

    own = lax.axis_index("expert").astype(i32).reshape(1)
    out_packed, logit_grad = call(
        lambda *refs: router_kernel(experts, *refs),
        (shape(main, features + 2 * part), shape(2, main, 128, kind=f32)),
        10**6,
        aliases={3: 0},
        grid=(1,),
        in_specs=[
            scalar,
            whole,
            whole,
            pl.BlockSpec((main, features + 2 * part), lambda i: (0, 0)),
        ],
        out_specs=(
            pl.BlockSpec((main, part), lambda i: (0, fold + 1)),
            pl.BlockSpec((2, main, 128), lambda i: (0, 0, 0)),
        ),
        scratch_shapes=[pltpu.VMEM((experts, fold, part), f32)],
    )(own, cot_arrived, arrived, out_packed)
    out_packed, cot_arrived, hidden, row_block, logit_grad = lax.optimization_barrier(
        (out_packed, cot_arrived, hidden, row_block, logit_grad)
    )
    out_back = exchange(out_packed, experts)

    joined, grads = call(
        lambda *refs: hidden_kernel(experts, *refs),
        (shape(slots, 2 * hidden_units), shape(slots, features)),
        10**6,
    )(cot_arrived, projected, down)
    both = call(
        grads_kernel,
        shape(features, 3 * hidden_units),
        10**6,
        grid=(fold,),
        in_specs=[
            pl.BlockSpec((slots, part), lambda i: (0, i)),
            pl.BlockSpec((slots, 2 * hidden_units), lambda i: (0, 0)),
            pl.BlockSpec((slots, part), lambda i: (0, i)),
            pl.BlockSpec((slots, hidden_units), lambda i: (0, 0)),
        ],
        out_specs=pl.BlockSpec((part, 3 * hidden_units), lambda i: (i, 0)),
    )(row_block, joined, grads, hidden)
    both = lax.psum_scatter(both, "dp", scatter_dimension=0, tiled=True)
    rows_packed = call(
        lambda *refs: rows_kernel(experts, *refs),
        shape(main, features + part),
        10**6,
        grid=(fold + 1,),
        in_specs=[
            pl.BlockSpec((slots, 2 * hidden_units), lambda i: (0, 0)),
            pl.BlockSpec((part, 2 * hidden_units), lambda i: (jnp.minimum(i, fold - 1), 0)),
            pl.BlockSpec((2, main, 128), lambda i: (0, 0, 0)),
            pl.BlockSpec((experts, part), lambda i: (0, jnp.minimum(i, fold - 1))),
        ],
        out_specs=pl.BlockSpec((main, part), lambda i: (0, i)),
        scratch_shapes=[
            pltpu.VMEM((main, part), f32),
            pltpu.VMEM((2 * main, 3 * experts), bf16),
        ],
    )(joined, weights, logit_grad, router)
    router_part = call(
        reduce_kernel,
        shape(fold, part, kind=f32),
        300000 * 10**6,
        grid=(1,),
        in_specs=[pl.BlockSpec((main, part), lambda i: (0, fold + 1))],
        out_specs=pl.BlockSpec((fold, part), lambda i: (0, 0)),
    )(out_back)
    rows_packed, router_part = lax.optimization_barrier((rows_packed, router_part))
    rows_back = exchange(rows_packed, experts)
    copies = lax.axis_size("dp")
    flips = [1] + [flip for flip in range(2, copies, 2)]
    router_part = router_part + (swap(router_part, "dp", 1) if copies > 1 else 0.0)
    parts = [swap(router_part, "dp", flip) for flip in flips[1:]]
    router_all = sum(parts, router_part)[None]
    upper_input = call(upper_kernel, shape(tokens, features, kind=f32), 10**6)(
        upper_out, out_back, mix
    )
    for flips in rounds(experts):
        parts = [swap(router_all, "expert", flip) for flip in flips]
        router_all = jnp.concatenate([router_all, *parts], axis=0)
    router_grad = call(
        lambda own, parts, out: order_kernel(experts, own, parts, out),
        shape(experts, features, kind=f32),
        10**6,
        in_specs=[scalar, whole],
        out_specs=whole,
    )(own, router_all).T
    lower_grad = call(lower_kernel, shape(tokens, features, kind=f32), 10**6)(
        lower_cot, rows_back, used
    )
    lower_grad, both = lax.optimization_barrier((lower_grad, both))
    gate_up_grad, down_grad = call(
        split_kernel,
        (shape(both.shape[0], 2 * hidden_units), shape(hidden_units, both.shape[0])),
        10**6,
    )(both)
    return upper_input, lower_grad, gate_up_grad[None], down_grad.T[None], router_grad


def solution(mesh):
    blocks = P(("expert", "dp"), None)
    split = P("expert", "dp", None)
    return jax.shard_map(
        body,
        mesh=mesh,
        in_specs=(blocks, blocks, blocks, blocks, split, split, P(), blocks, blocks),
        out_specs=(blocks, blocks, split, split, P()),
        check_vma=False,
    )
```
